32 devices in a mesh: lon: 8 (over z, x), lat: 4 (over y, core).
Axes of the slice: x: 2, y: 2, z: 4, core: 2. Of those that a mesh axis runs over, the one named last changes fastest.
Arguments:
- state: float32 [4, 4, 128, 2048], P(None, None, 'lat', 'lon'), may hold values from -3 to 3
- cotangent: float32 [4, 4, 128, 2048], P(None, None, 'lat', 'lon'), may hold values from -6 to 6
- seamask: int32 [128, 2048], P('lat', 'lon'), may hold values 0 or 1
- levels: int32 [128, 2048], P('lat', 'lon'), may hold values from 1 to 4
Outputs:
- final_state: float32 [4, 4, 128, 2048], P(None, None, 'lat', 'lon')
- adjoint_state: float32 [4, 4, 128, 2048], P(None, None, 'lat', 'lon')
The draws below stay inside these ranges and needn't reach their ends.
All inputs are finite; a program needn't handle non-finite values. No bound on the sum of `seamask` on one device may be relied on, other than what follows from the above.
Results may differ from the reference program's by a relative error of at most 0.0003.
Values sent between devices are 32-bit elements; how exact they have to be, the bound alone decides.
A program may use at most 64 MiB of HBM per device.

```python
import jax
import jax.numpy as jnp
from jax import lax

LEV = 4
CLAT = 32
NLAT = 128
NLON = 2048
N_LAT = 4


def with_ends(result, key, smallest, top_value):
    shape = result.shape
    place = [jax.random.randint(jax.random.fold_in(key, axis), (), 0, shape[axis]) for axis in range(len(shape))]
    result = result.at[tuple(place)].set(smallest)
    longest = shape.index(max(shape))
    place[longest] = (place[longest] + 1) % shape[longest]
    return result.at[tuple(place)].set(top_value)


def shard_levels(own_key, shape, shards, least, high):
    level = 1.0
    for position, shards_of in shards:
        heights = jax.random.uniform(jax.random.fold_in(jax.random.fold_in(own_key, 6), position), (shards_of,), jnp.float32, least / len(shards), high / len(shards))
        level = level * jnp.repeat(jnp.exp(heights), shape[position] // shards_of).reshape((-1,) + (1,) * (len(shape) - 1 - position))
    return level


def noise(stream_key, shape, spread, limit, pieces=(), held_as=jnp.bfloat16):
    gain = shard_levels(stream_key, shape, pieces, -0.22, 0.18) if pieces else 1.0
    result = jax.random.normal(stream_key, shape, jnp.float32) * spread * gain
    return jnp.minimum(jnp.maximum(result, -limit), limit).astype(held_as)


def setup_inputs(seed: int = 0) -> dict:
    key_of = jax.random.split(jax.random.key(seed), 5)
    state = noise(key_of[0], (4, LEV, NLAT, NLON), 0.5, 3.0, ((2, 4), (3, 8)), jnp.float32)
    cotangent = noise(key_of[1], (4, LEV, NLAT, NLON), 1.0, 6.0, ((2, 4), (3, 8)), jnp.float32)
    seamask = with_ends((jax.random.randint(key_of[2], (NLAT, NLON), 0, 5) < 4).astype(jnp.int32), jax.random.fold_in(key_of[2], 1), 0, 1)
    levels = with_ends(jax.random.randint(key_of[3], (NLAT, NLON), 1, LEV + 1), jax.random.fold_in(key_of[3], 1), 1, LEV).astype(jnp.int32)
    return {"state": state, "cotangent": cotangent, "seamask": seamask, "levels": levels}


courant = 0.4
vert_mix = 0.1
rotation = 0.3
buoyancy = 0.3
bottom_drag = 0.2

def slab_of(values, start, length, along):
    return lax.slice_in_dim(values, start, start + length, axis=values.ndim + along)

def face_div(fields, speeds, wet_mask, along):
    extent = fields.shape[along]
    faces = extent - 5
    cells = [slab_of(fields, offset, faces, along) for offset in range(6)]
    face_speed = 0.5 * (slab_of(speeds, 2, faces, along) + slab_of(speeds, 3, faces, along))
    open_face = slab_of(wet_mask, 2, faces, along) * slab_of(wet_mask, 3, faces, along)
    central = (37.0 * (cells[2] + cells[3]) - 8.0 * (cells[1] + cells[4]) + (cells[0] + cells[5])) / 60.0
    damping = (10.0 * (cells[3] - cells[2]) - 5.0 * (cells[4] - cells[1]) + (cells[5] - cells[0])) / 60.0
    flux = open_face * (face_speed * central - jnp.sqrt(face_speed * face_speed + 0.0001) * damping)
    return slab_of(flux, 1, faces - 1, along) - slab_of(flux, 0, faces - 1, along)

def advance(padded, sea_rim, level_rim, first_row, lat_total):
    level_count = padded.shape[1]
    lat_cells = padded.shape[2]
    lon_cells = padded.shape[3]
    level_index = jnp.arange(level_count, dtype=jnp.int32)[:, None, None]
    wet_mask = (sea_rim[None] * (level_index < level_rim[None]).astype(jnp.int32)).astype(jnp.float32)
    bottom = (sea_rim[None] * (level_index == level_rim[None] - 1).astype(jnp.int32)).astype(jnp.float32)
    divergence = face_div(padded, padded[2], wet_mask, -1)[:, :, 3:lat_cells - 3, :]
    divergence = divergence + face_div(padded, padded[3], wet_mask, -2)[:, :, :, 3:lon_cells - 3]
    center = padded[:, :, 3:lat_cells - 3, 3:lon_cells - 3]
    wet_center = wet_mask[:, 3:lat_cells - 3, 3:lon_cells - 3]
    bottom_center = bottom[:, 3:lat_cells - 3, 3:lon_cells - 3]
    zero_level = jnp.zeros_like(center[:, :1])
    zero_wet = jnp.zeros_like(wet_center[:1])
    above_cells = jnp.concatenate([zero_level, center[:, :-1]], axis=1)
    below_cells = jnp.concatenate([center[:, 1:], zero_level], axis=1)
    wet_above = jnp.concatenate([zero_wet, wet_center[:-1]], axis=0)
    wet_below = jnp.concatenate([wet_center[1:], zero_wet], axis=0)
    vertical = vert_mix * (wet_above * (above_cells - center) + wet_below * (below_cells - center))
    density = (-0.2 * padded[0] + 0.8 * padded[1]) * wet_mask
    pressure = buoyancy * jnp.cumsum(density, axis=0)
    press_east = 0.5 * (pressure[:, 3:lat_cells - 3, 4:lon_cells - 2] - pressure[:, 3:lat_cells - 3, 2:lon_cells - 4])
    press_north = 0.5 * (pressure[:, 4:lat_cells - 2, 3:lon_cells - 3] - pressure[:, 2:lat_cells - 4, 3:lon_cells - 3])
    row_index = (first_row + 3 + jnp.arange(lat_cells - 6, dtype=jnp.int32)).astype(jnp.float32)
    latitude = jnp.pi * ((row_index + 0.5) / lat_total - 0.5)
    coriolis = (rotation * jnp.sin(latitude))[:, None]
    east_now = center[2]
    north_now = center[3]
    force_east = coriolis * north_now - press_east - bottom_drag * bottom_center * east_now
    force_north = -coriolis * east_now - press_north - bottom_drag * bottom_center * north_now
    forcing = jnp.concatenate([jnp.zeros_like(center[:2]), jnp.stack([force_east, force_north])], axis=0)
    return (center - courant * divergence + vertical + forcing) * wet_center[None]

def wrap_lon(values, rim_width):
    return jnp.concatenate([values[..., -rim_width:], values, values[..., :rim_width]], axis=-1)

def reference(state, cotangent, seamask, levels):
    margin = 12
    lat_padded = jnp.pad(state, ((0, 0), (0, 0), (margin, margin), (0, 0)))
    cot_padded = jnp.pad(cotangent, ((0, 0), (0, 0), (6, 6), (0, 0)))
    sea_padded = jnp.pad(seamask, ((margin, margin), (0, 0)))
    lev_padded = jnp.pad(levels, ((margin, margin), (0, 0)))

    def one_block(block):
        start = (block * CLAT).astype(jnp.int32)
        slab = lax.dynamic_slice_in_dim(lat_padded, start, CLAT + 2 * margin, axis=2)
        sea_slab = wrap_lon(lax.dynamic_slice_in_dim(sea_padded, start, CLAT + 2 * margin, axis=0), 6)
        lev_slab = wrap_lon(lax.dynamic_slice_in_dim(lev_padded, start, CLAT + 2 * margin, axis=0), 6)
        cot_slab = lax.dynamic_slice_in_dim(cot_padded, start, CLAT + 12, axis=2)
        first_row = start - margin

        def two_steps(rows_in):
            half_way = advance(wrap_lon(rows_in, 6), sea_slab, lev_slab, first_row, NLAT)
            return advance(half_way, sea_slab[3:-3, 3:-3], lev_slab[3:-3, 3:-3], first_row + 3, NLAT)
        ahead, backward = jax.vjp(two_steps, slab)
        gradient = backward(cot_slab)[0]
        return (ahead[:, :, 6:6 + CLAT], gradient[:, :, margin:margin + CLAT])
    finals, grads = lax.map(one_block, jnp.arange(N_LAT, dtype=jnp.int32))
    final_state = jnp.moveaxis(finals, 0, 2).reshape(4, LEV, NLAT, NLON)
    adjoint_state = jnp.moveaxis(grads, 0, 2).reshape(4, LEV, NLAT, NLON)
    return (final_state, adjoint_state)
```

```python
import functools

import jax
import jax.numpy as jnp
from jax import lax
from jax.experimental import pallas as pl
from jax.experimental.pallas import tpu as pltpu
from jax.sharding import PartitionSpec as P

courant = 0.4
vert_mix = 0.1
rotation = 0.3
buoyancy = 0.3
bottom_drag = 0.2

LANES = 128
RIM = 16
MESH = pl.DeviceIdType.MESH


def exchange_kernel(state, cot, sea, lev, rows_s, rows_c, rows_n, strips, pack, depth, send, recv):
    planes, rows, cols = state.shape
    lon = lax.axis_index("lon")
    lat = lax.axis_index("lat")
    lon_n = lax.axis_size("lon")
    lat_n = lax.axis_size("lat")
    left = lax.rem(lon + lon_n - 1, lon_n)
    right = lax.rem(lon + 1, lon_n)
    has_up = lat > 0
    has_down = lat < lat_n - 1

    barrier = pltpu.get_barrier_semaphore()

    def greet(to_lon, to_lat):
        pl.semaphore_signal(barrier, inc=1, device_id=(to_lon, to_lat), device_id_type=MESH)

    greet(left, lat)
    greet(right, lat)

    @pl.when(has_up)
    def _():
        for to_lon in (left, lon, right):
            greet(to_lon, lat - 1)

    @pl.when(has_down)
    def _():
        for to_lon in (left, lon, right):
            greet(to_lon, lat + 1)

    depth[...] = (sea[...] * lev[...]).astype(jnp.float32)
    lane = lax.broadcasted_iota(jnp.int32, (rows, LANES), 1)
    for side in range(2):
        part = slice(0, LANES) if side == 0 else slice(cols - LANES, cols)
        for half in range(2):
            total = jnp.zeros((rows, LANES), jnp.float32)
            for slot in range(8):
                origin = 0 if side == 0 else LANES - 16
                moved = pltpu.roll(state[half * 8 + slot, :, part], (16 * slot - origin) % LANES, 1)
                total = jnp.where(lane // 16 == slot, moved, total)
            pack[side, :, half * LANES : (half + 1) * LANES] = total
        total = jnp.zeros((rows, LANES), jnp.float32)
        for slot in range(16):
            origin = 0 if side == 0 else LANES - 8
            moved = pltpu.roll(cot[slot, :, part], (8 * slot - origin) % LANES, 1)
            total = jnp.where(lane // 8 == slot, moved, total)
        pack[side, :, 2 * LANES : 3 * LANES] = total
        pack[side, :, 3 * LANES : 4 * LANES] = depth[:, part]

    sides = jnp.where(has_up, 1, 0) + jnp.where(has_down, 1, 0)
    pl.semaphore_wait(barrier, 2 + 3 * sides)

    def message(number, source, target, to_lon, to_lat):
        return pltpu.make_async_remote_copy(
            src_ref=source,
            dst_ref=target,
            send_sem=send.at[number],
            recv_sem=recv.at[number],
            device_id=(to_lon, to_lat),
            device_id_type=MESH,
        )

    end = rows + RIM
    sideways = [
        message(0, pack.at[0], strips.at[0, RIM:end], left, lat),
        message(1, pack.at[1], strips.at[1, RIM:end], right, lat),
    ]
    up = [
        message(2, state.at[:, 0:RIM], rows_s.at[1], lon, lat - 1),
        message(3, cot.at[:, 0:8], rows_c.at[1], lon, lat - 1),
        message(4, depth.at[0:8], rows_n.at[1], lon, lat - 1),
        message(5, pack.at[0, 0:RIM], strips.at[0, end : end + RIM], left, lat - 1),
        message(6, pack.at[1, 0:RIM], strips.at[1, end : end + RIM], right, lat - 1),
    ]
    down = [
        message(7, state.at[:, rows - RIM : rows], rows_s.at[0], lon, lat + 1),
        message(8, cot.at[:, rows - 8 : rows], rows_c.at[0], lon, lat + 1),
        message(9, depth.at[rows - 8 : rows], rows_n.at[0], lon, lat + 1),
        message(10, pack.at[0, rows - RIM : rows], strips.at[0, 0:RIM], left, lat + 1),
        message(11, pack.at[1, rows - RIM : rows], strips.at[1, 0:RIM], right, lat + 1),
    ]

    @pl.when(has_up)
    def _():
        for copy in up:
            copy.start()

    @pl.when(has_down)
    def _():
        for copy in down:
            copy.start()

    for copy in sideways:
        copy.start()
    for copy in sideways:
        copy.wait()

    @pl.when(has_up)
    def _():
        for copy in up:
            copy.wait_send()
        for copy in down:
            copy.wait_recv()

    @pl.when(has_down)
    def _():
        for copy in down:
            copy.wait_send()
        for copy in up:
            copy.wait_recv()


def exchange(state, cot, sea, lev):
    planes, rows, cols = state.shape
    f32 = jnp.float32
    return pl.pallas_call(
        exchange_kernel,
        out_shape=(
            jax.ShapeDtypeStruct((2, planes, RIM, cols), f32),
            jax.ShapeDtypeStruct((2, planes, 8, cols), f32),
            jax.ShapeDtypeStruct((2, 8, cols), f32),
            jax.ShapeDtypeStruct((2, rows + 2 * RIM, 4 * LANES), f32),
        ),
        in_specs=[pl.BlockSpec(memory_space=pltpu.VMEM)] * 4,
        out_specs=[pl.BlockSpec(memory_space=pl.ANY)] * 4,
        scratch_shapes=[
            pltpu.VMEM((2, rows, 4 * LANES), f32),
            pltpu.VMEM((rows, cols), f32),
            pltpu.SemaphoreType.DMA((12,)),
            pltpu.SemaphoreType.DMA((12,)),
        ],
        compiler_params=pltpu.CompilerParams(collective_id=0, has_side_effects=True),
        name="exchange",
    )(state, cot, sea, lev)


def step_kernel(
    lat_n, state, cot, sea, lev, rows_s, rows_c, rows_n, strips, final, adjoint,
    S, G, X1, X2, A1, FA, FB, KX, KY, WET, BOT, OX, OY, PR, W, LWY, COR,
):
    planes, rows, cols = state.shape
    levels = WET.shape[0]
    tall = rows + 2 * RIM
    tiles = cols // LANES + 1
    lat = lax.axis_index("lat")
    lane = lax.broadcasted_iota(jnp.int32, (tiles, 8, LANES), 2)
    flat_lane = lax.broadcasted_iota(jnp.int32, (8, LANES), 1)
    lat_vec = jnp.full((8, LANES), lat, jnp.int32)

    def east(v, d):
        rolled = pltpu.roll(v, (-d) % LANES, 2)
        if d > 0:
            other = jnp.concatenate([rolled[1:], rolled[:1]], axis=0)
            return jnp.where(lane < LANES - d, rolled, other)
        other = jnp.concatenate([rolled[-1:], rolled[:-1]], axis=0)
        return jnp.where(lane >= -d, rolled, other)

    def at(ref, p, r):
        return ref[p, :, pl.ds(r, 8), :]

    def put(ref, p, r, v):
        ref[p, :, pl.ds(r, 8), :] = v

    for t in range(tall // 8):
        r = 8 * t
        own = RIM <= r < rows + RIM
        slot = 0 if r < RIM else 1
        edge = (lat_vec > 0) if r < RIM else (lat_vec < lat_n - 1)

        def inside(v):
            return v if own else jnp.where(edge, v, 0.0)

        def third(tile, width, place):
            right = pltpu.roll(strips[0, r : r + 8, tile], (-width * place) % LANES, 1)
            if width * place == 0:
                right = strips[0, r : r + 8, tile]
            shift = (LANES - width - width * place) % LANES
            left = strips[1, r : r + 8, tile]
            if shift:
                left = pltpu.roll(left, shift, 1)
            return jnp.where(flat_lane < 64, right, left)

        near = RIM - 8 <= r < rows + RIM + 8
        if near:
            for j in range(tiles - 1):
                part = slice(j * LANES, (j + 1) * LANES)
                if own:
                    depth = (sea[r - RIM : r - RIM + 8, part] * lev[r - RIM : r - RIM + 8, part]).astype(
                        jnp.float32
                    )
                else:
                    depth = inside(rows_n[slot, :, part])
                for k in range(levels):
                    WET[k, j, r : r + 8, :] = (depth > k + 0.5).astype(jnp.float32)
                    BOT[k, j, r : r + 8, :] = jnp.where(jnp.abs(depth - (k + 1)) < 0.5, 1.0, 0.0)
            depth = inside(
                jnp.where(
                    flat_lane < 64,
                    strips[0, r : r + 8, 3 * LANES : 4 * LANES],
                    strips[1, r : r + 8, 3 * LANES : 4 * LANES],
                )
            )
            for k in range(levels):
                WET[k, tiles - 1, r : r + 8, :] = (depth > k + 0.5).astype(jnp.float32)
                BOT[k, tiles - 1, r : r + 8, :] = jnp.where(jnp.abs(depth - (k + 1)) < 0.5, 1.0, 0.0)
        else:
            for k in range(levels):
                WET[k, :, r : r + 8, :] = jnp.zeros((tiles, 8, LANES), jnp.float32)
        for p in range(planes):
            k = p % levels
            for j in range(tiles - 1):
                part = slice(j * LANES, (j + 1) * LANES)
                if own:
                    S[p, j, r : r + 8, :] = state[p, r - RIM : r - RIM + 8, part]
                    G[p, j, r : r + 8, :] = WET[k, j, r : r + 8, :] * cot[p, r - RIM : r - RIM + 8, part]
                else:
                    base = r if slot == 0 else r - rows - RIM
                    S[p, j, r : r + 8, :] = inside(rows_s[slot, p, base : base + 8, part])
                    if near:
                        G[p, j, r : r + 8, :] = WET[k, j, r : r + 8, :] * inside(rows_c[slot, p, :, part])
            half = p // 8
            S[p, tiles - 1, r : r + 8, :] = inside(
                third(slice(half * LANES, (half + 1) * LANES), 16, p % 8)
            )
            if near:
                G[p, tiles - 1, r : r + 8, :] = WET[k, tiles - 1, r : r + 8, :] * inside(
                    third(slice(2 * LANES, 3 * LANES), 8, p)
                )

    row = lax.broadcasted_iota(jnp.int32, (tall, LANES), 0) + (lat * rows - RIM)
    turn = jnp.pi * ((row.astype(jnp.float32) + 0.5) / (rows * lat_n) - 0.5)
    COR[...] = rotation * jnp.sin(turn)

    def sweep(first, count, body):
        def run(i, carry):
            body(first + 8 * i)
            return carry

        lax.fori_loop(0, count, run, 0)

    inner = rows // 8

    def open_faces(r):
        for k in range(levels):
            wet = at(WET, k, r)
            put(OX, k, r, wet * east(wet, 1) * (courant / 60.0))
            put(OY, k, r, wet * at(WET, k, r + 1) * (courant / 60.0))

    sweep(8, inner + 2, open_faces)

    def prepare(src, step):
        def body(r):
            press = None
            for k in range(levels):
                rho = at(WET, k, r) * (
                    (-0.2 * buoyancy) * at(src, k, r) + (0.8 * buoyancy) * at(src, levels + k, r)
                )
                press = rho if press is None else press + rho
                put(PR, k, r, press)
                u = at(src, 2 * levels + k, r)
                w = 0.5 * (u + east(u, 1))
                put(W, (step * 6) * levels + k, r, w)
                square = w * w + 0.0001
                root = lax.rsqrt(square)
                put(W, (step * 6 + 1) * levels + k, r, square * root)
                put(W, (step * 6 + 2) * levels + k, r, w * root)
                w = 0.5 * (at(src, 3 * levels + k, r) + at(src, 3 * levels + k, r + 1))
                put(W, (step * 6 + 3) * levels + k, r, w)
                square = w * w + 0.0001
                root = lax.rsqrt(square)
                put(W, (step * 6 + 4) * levels + k, r, square * root)
                put(W, (step * 6 + 5) * levels + k, r, w * root)

        sweep(8, inner + 2, body)

    def speeds(step, k, r, along):
        base = step * 6 + 3 * along
        return [at(W, (base + i) * levels + k, r) for i in range(3)]

    def stencil(c0, c1, c2, c3, c4, c5):
        central = 37.0 * (c2 + c3) - 8.0 * (c1 + c4) + (c0 + c5)
        damping = 10.0 * (c3 - c2) - 5.0 * (c4 - c1) + (c5 - c0)
        return central, damping

    def forward(src, dst, step, first, count):
        prepare(src, step)

        def body(r):
            turn = COR[pl.ds(r, 8), :][None]

            def level(k, carry):
                wet = at(WET, k, r)
                ox = at(OX, k, r)
                oy = at(OY, k, r)
                wx, sx, tx = speeds(step, k, r, 0)
                wy, sy, ty = speeds(step, k, r, 1)
                lo = jnp.maximum(k - 1, 0)
                hi = jnp.minimum(k + 1, levels - 1)
                mix_lo = vert_mix * at(WET, lo, r)
                mix_hi = vert_mix * at(WET, hi, r)
                for f in range(4):
                    p = f * levels + k
                    q = at(src, p, r)
                    c, d = stencil(east(q, -2), east(q, -1), q, east(q, 1), east(q, 2), east(q, 3))
                    put(KX, step * planes + p, r, c - tx * d)
                    flux = ox * (wx * c - sx * d)
                    total = q - (flux - east(flux, -1))
                    c, d = stencil(*[at(src, p, r + o) for o in (-2, -1)], q, *[at(src, p, r + o) for o in (1, 2, 3)])
                    put(KY, step * planes + p, r, c - ty * d)
                    flux = oy * (wy * c - sy * d)
                    put(FA, p, r, flux)
                    total = total - (flux - at(FA, p, r - 1))
                    total = total + mix_lo * (at(src, f * levels + lo, r) - q)
                    total = total + mix_hi * (at(src, f * levels + hi, r) - q)
                    if f == 2:
                        press = at(PR, k, r)
                        total = total + turn * at(src, 3 * levels + k, r)
                        total = total - 0.5 * (east(press, 1) - east(press, -1))
                        total = total - bottom_drag * at(BOT, k, r) * q
                    if f == 3:
                        total = total - turn * at(src, 2 * levels + k, r)
                        total = total - 0.5 * (at(PR, k, r + 1) - at(PR, k, r - 1))
                        total = total - bottom_drag * at(BOT, k, r) * q
                    put(dst, p, r, wet * total)
                return carry

            lax.fori_loop(0, levels, level, 0)

        sweep(first, count, body)

    def backward(grad, step, first_face, faces, first, count, store):
        def face_body(r):
            def level(k, carry):
                oy = at(OY, k, r)
                wy, sy, _ = speeds(step, k, r, 1)
                by_speed = None
                for f in range(4):
                    p = f * levels + k
                    h = oy * (at(grad, p, r + 1) - at(grad, p, r))
                    put(FA, p, r, wy * h)
                    put(FB, p, r, sy * h)
                    term = h * at(KY, step * planes + p, r)
                    by_speed = term if by_speed is None else by_speed + term
                put(LWY, k, r, by_speed)
                return carry

            lax.fori_loop(0, levels, level, 0)

        sweep(first_face, faces, face_body)

        def body(r):
            turn = COR[pl.ds(r, 8), :][None]

            def level(i, below):
                k = levels - 1 - i
                wet = at(WET, k, r)
                ox = at(OX, k, r)
                wx, sx, _ = speeds(step, k, r, 0)
                lo = jnp.maximum(k - 1, 0)
                hi = jnp.minimum(k + 1, levels - 1)
                mix_wet = vert_mix * wet
                wet_lo = jnp.where(k > 0, 1.0, 0.0) * vert_mix * at(WET, lo, r)
                wet_hi = jnp.where(k < levels - 1, 1.0, 0.0) * vert_mix * at(WET, hi, r)
                has_lo = jnp.where(k > 0, 1.0, 0.0) * mix_wet
                has_hi = jnp.where(k < levels - 1, 1.0, 0.0) * mix_wet
                keep = 1.0 - wet_lo - wet_hi
                gu = at(grad, 2 * levels + k, r)
                gv = at(grad, 3 * levels + k, r)
                by_press = 0.5 * (east(gu, 1) - east(gu, -1)) + 0.5 * (
                    at(grad, 3 * levels + k, r + 1) - at(grad, 3 * levels + k, r - 1)
                )
                below = below + by_press
                by_rho = buoyancy * wet * below
                drag = bottom_drag * at(BOT, k, r)
                speed_x = None
                sums = []
                for f in range(4):
                    p = f * levels + k
                    g = at(grad, p, r)
                    total = keep * g + has_lo * at(grad, f * levels + lo, r) + has_hi * at(grad, f * levels + hi, r)
                    h = ox * (east(g, 1) - g)
                    term = h * at(KX, step * planes + p, r)
                    speed_x = term if speed_x is None else speed_x + term
                    zw = wx * h
                    zs = sx * h
                    lr = zw + east(zw, -1)
                    le = zs - east(zs, -1)
                    both = lr + le
                    near = -9.0 * lr - 4.0 * le
                    total = total + (46.0 * lr + 6.0 * le) + (east(near, 1) + east(near, -1))
                    total = total + (east(both, 2) + east(both, -2))
                    z = [at(FA, p, r + o) for o in range(-3, 3)]
                    total = total + (37.0 * (z[2] + z[3]) - 8.0 * (z[1] + z[4]) + (z[0] + z[5]))
                    z = [at(FB, p, r + o) for o in range(-3, 3)]
                    total = total + (10.0 * (z[3] - z[2]) - 5.0 * (z[4] - z[1]) + (z[5] - z[0]))
                    sums.append(total)
                speed_y = at(LWY, k, r) + at(LWY, k, r - 1)
                sums[0] = sums[0] - 0.2 * by_rho
                sums[1] = sums[1] + 0.8 * by_rho
                sums[2] = sums[2] + 0.5 * (speed_x + east(speed_x, -1)) - turn * gv - drag * gu
                sums[3] = sums[3] + 0.5 * speed_y + turn * gu - drag * gv
                for f in range(4):
                    store(f * levels + k, r, sums[f], wet)
                return below

            lax.fori_loop(0, levels, level, jnp.zeros((tiles, 8, LANES), jnp.float32))

        sweep(first, count, body)

    forward(S, X1, 0, 8, inner + 2)
    forward(X1, X2, 1, RIM - 4, inner + 1)

    def store_middle(p, r, v, wet):
        put(A1, p, r, wet * v)

    def store_last(p, r, v, wet):
        row = pl.multiple_of(r - RIM, 8)
        for j in range(tiles - 1):
            adjoint[p, pl.ds(row, 8), j * LANES : (j + 1) * LANES] = v[j]

    backward(G, 1, 8, inner + 2, RIM - 4, inner + 1, store_middle)
    backward(A1, 0, RIM - 4, inner + 1, RIM, inner, store_last)
    for p in range(planes):
        for j in range(tiles - 1):
            final[p, :, j * LANES : (j + 1) * LANES] = X2[p, j, RIM : RIM + rows, :]


def steps(lat_n, state, cot, sea, lev, halos):
    planes, rows, cols = state.shape
    levels = planes // 4
    f32 = jnp.float32
    tall = rows + 2 * RIM
    tiles = cols // LANES + 1

    def scratch(count):
        return pltpu.VMEM((count, tiles, tall, LANES), f32)

    counts = [planes] * 7 + [2 * planes] * 2 + [levels] * 5 + [12 * levels, levels]
    return pl.pallas_call(
        functools.partial(step_kernel, lat_n),
        out_shape=(jax.ShapeDtypeStruct(state.shape, f32),) * 2,
        in_specs=[pl.BlockSpec(memory_space=pltpu.VMEM)] * 8,
        out_specs=(pl.BlockSpec(memory_space=pltpu.VMEM),) * 2,
        scratch_shapes=[scratch(count) for count in counts] + [pltpu.VMEM((tall, LANES), f32)],
        compiler_params=pltpu.CompilerParams(vmem_limit_bytes=56 * 1024 * 1024),
        name="steps",
    )(state, cot, sea, lev, *halos)


def shards(state, cotangent, seamask, levels):
    shape = state.shape
    flat = (shape[0] * shape[1], shape[2], shape[3])
    state = state.reshape(flat)
    cotangent = cotangent.reshape(flat)
    halos = exchange(state, cotangent, seamask, levels)
    final, adjoint = steps(lax.axis_size("lat"), state, cotangent, seamask, levels, halos)
    return (final.reshape(shape), adjoint.reshape(shape))


def solution(mesh):
    placed = (
        P(None, None, "lat", "lon"),
        P(None, None, "lat", "lon"),
        P("lat", "lon"),
        P("lat", "lon"),
    )
    return jax.shard_map(
        shards,
        mesh=mesh,
        in_specs=placed,
        out_specs=(P(None, None, "lat", "lon"), P(None, None, "lat", "lon")),
        check_vma=False,
    )
```

```python
import functools

import jax
import jax.numpy as jnp
import numpy as np
from jax import lax
from jax.experimental import pallas as pl
from jax.experimental.pallas import tpu as pltpu
from jax.sharding import PartitionSpec as P

courant = 0.4
vert_mix = 0.1
rotation = 0.3
buoyancy = 0.3
bottom_drag = 0.2

LANES = 128
RIM = 16
MESH = pl.DeviceIdType.MESH


def exchange_kernel(state, cot, sea, lev, rows_s, rows_c, rows_n, strips, pack, depth, send, recv):
    planes, rows, cols = state.shape
    lon = lax.axis_index("lon")
    lat = lax.axis_index("lat")
    lon_n = lax.axis_size("lon")
    lat_n = lax.axis_size("lat")
    left = lax.rem(lon + lon_n - 1, lon_n)
    right = lax.rem(lon + 1, lon_n)
    has_up = lat > 0
    has_down = lat < lat_n - 1

    barrier = pltpu.get_barrier_semaphore()

    def greet(to_lon, to_lat):
        pl.semaphore_signal(barrier, inc=1, device_id=(to_lon, to_lat), device_id_type=MESH)

    greet(left, lat)
    greet(right, lat)

    @pl.when(has_up)
    def _():
        for to_lon in (left, lon, right):
            greet(to_lon, lat - 1)

    @pl.when(has_down)
    def _():
        for to_lon in (left, lon, right):
            greet(to_lon, lat + 1)

    depth[...] = (sea[...] * lev[...]).astype(jnp.float32)
    lane = lax.broadcasted_iota(jnp.int32, (rows, LANES), 1)
    for side in range(2):
        part = slice(0, LANES) if side == 0 else slice(cols - LANES, cols)
        for half in range(2):
            total = jnp.zeros((rows, LANES), jnp.float32)
            for slot in range(8):
                origin = 0 if side == 0 else LANES - 16
                moved = pltpu.roll(state[half * 8 + slot, :, part], (16 * slot - origin) % LANES, 1)
                total = jnp.where(lane // 16 == slot, moved, total)
            pack[side, :, half * LANES : (half + 1) * LANES] = total
        total = jnp.zeros((rows, LANES), jnp.float32)
        for slot in range(16):
            origin = 0 if side == 0 else LANES - 8
            moved = pltpu.roll(cot[slot, :, part], (8 * slot - origin) % LANES, 1)
            total = jnp.where(lane // 8 == slot, moved, total)
        pack[side, :, 2 * LANES : 3 * LANES] = total
        pack[side, :, 3 * LANES : 4 * LANES] = depth[:, part]

    sides = jnp.where(has_up, 1, 0) + jnp.where(has_down, 1, 0)
    pl.semaphore_wait(barrier, 2 + 3 * sides)

    def message(number, source, target, to_lon, to_lat):
        return pltpu.make_async_remote_copy(
            src_ref=source,
            dst_ref=target,
            send_sem=send.at[number],
            recv_sem=recv.at[number],
            device_id=(to_lon, to_lat),
            device_id_type=MESH,
        )

    end = rows + RIM
    sideways = [
        message(0, pack.at[0], strips.at[0, RIM:end], left, lat),
        message(1, pack.at[1], strips.at[1, RIM:end], right, lat),
    ]
    up = [
        message(2, state.at[:, 0:RIM], rows_s.at[1], lon, lat - 1),
        message(3, cot.at[:, 0:8], rows_c.at[1], lon, lat - 1),
        message(4, depth.at[0:8], rows_n.at[1], lon, lat - 1),
        message(5, pack.at[0, 0:RIM], strips.at[0, end : end + RIM], left, lat - 1),
        message(6, pack.at[1, 0:RIM], strips.at[1, end : end + RIM], right, lat - 1),
    ]
    down = [
        message(7, state.at[:, rows - RIM : rows], rows_s.at[0], lon, lat + 1),
        message(8, cot.at[:, rows - 8 : rows], rows_c.at[0], lon, lat + 1),
        message(9, depth.at[rows - 8 : rows], rows_n.at[0], lon, lat + 1),
        message(10, pack.at[0, rows - RIM : rows], strips.at[0, 0:RIM], left, lat + 1),
        message(11, pack.at[1, rows - RIM : rows], strips.at[1, 0:RIM], right, lat + 1),
    ]

    @pl.when(has_up)
    def _():
        for copy in up:
            copy.start()

    @pl.when(has_down)
    def _():
        for copy in down:
            copy.start()

    for copy in sideways:
        copy.start()
    for copy in sideways:
        copy.wait()

    @pl.when(has_up)
    def _():
        for copy in up:
            copy.wait_send()
        for copy in down:
            copy.wait_recv()

    @pl.when(has_down)
    def _():
        for copy in down:
            copy.wait_send()
        for copy in up:
            copy.wait_recv()


def exchange(state, cot, sea, lev):
    planes, rows, cols = state.shape
    f32 = jnp.float32
    return pl.pallas_call(
        exchange_kernel,
        out_shape=(
            jax.ShapeDtypeStruct((2, planes, RIM, cols), f32),
            jax.ShapeDtypeStruct((2, planes, 8, cols), f32),
            jax.ShapeDtypeStruct((2, 8, cols), f32),
            jax.ShapeDtypeStruct((2, rows + 2 * RIM, 4 * LANES), f32),
        ),
        in_specs=[pl.BlockSpec(memory_space=pltpu.VMEM)] * 4,
        out_specs=[pl.BlockSpec(memory_space=pl.ANY)] * 4,
        scratch_shapes=[
            pltpu.VMEM((2, rows, 4 * LANES), f32),
            pltpu.VMEM((rows, cols), f32),
            pltpu.SemaphoreType.DMA((12,)),
            pltpu.SemaphoreType.DMA((12,)),
        ],
        compiler_params=pltpu.CompilerParams(collective_id=0, has_side_effects=True),
        name="exchange",
    )(state, cot, sea, lev)


def step_kernel(
    lat_n, state, cot, sea, lev, rows_s, rows_c, rows_n, strips, ahead, behind, final, adjoint,
    S, G, X1, X2, A1, FA, FB, LX, KX, KY, CD, WET, BOT, OX, OY, PR, W, LWY, LWX, COR, QB, ZB,
):
    planes, rows, cols = state.shape
    levels = WET.shape[0]
    tall = rows + 2 * RIM
    tiles = cols // LANES + 1
    lat = lax.axis_index("lat")
    lanes = {n: lax.broadcasted_iota(jnp.int32, (tiles, n, LANES), 2) for n in (8, 16)}
    flat_lane = lax.broadcasted_iota(jnp.int32, (8, LANES), 1)
    lat_vec = jnp.full((8, LANES), lat, jnp.int32)

    def east(v, d):
        lane = lanes[v.shape[1]]
        rolled = pltpu.roll(v, (-d) % LANES, 2)
        if d > 0:
            other = jnp.concatenate([rolled[1:], rolled[:1]], axis=0)
            return jnp.where(lane < LANES - d, rolled, other)
        other = jnp.concatenate([rolled[-1:], rolled[:-1]], axis=0)
        return jnp.where(lane >= -d, rolled, other)

    def at(ref, p, r):
        return ref[p, :, pl.ds(r, 8), :]

    def put(ref, p, r, v):
        ref[p, :, pl.ds(r, 8), :] = v

    for t in range(tall // 8):
        r = 8 * t
        own = RIM <= r < rows + RIM
        slot = 0 if r < RIM else 1
        edge = (lat_vec > 0) if r < RIM else (lat_vec < lat_n - 1)

        def inside(v):
            return v if own else jnp.where(edge, v, 0.0)

        def third(tile, width, place):
            right = pltpu.roll(strips[0, r : r + 8, tile], (-width * place) % LANES, 1)
            if width * place == 0:
                right = strips[0, r : r + 8, tile]
            shift = (LANES - width - width * place) % LANES
            left = strips[1, r : r + 8, tile]
            if shift:
                left = pltpu.roll(left, shift, 1)
            return jnp.where(flat_lane < 64, right, left)

        near = RIM - 8 <= r < rows + RIM + 8
        if near:
            for j in range(tiles - 1):
                part = slice(j * LANES, (j + 1) * LANES)
                if own:
                    depth = (sea[r - RIM : r - RIM + 8, part] * lev[r - RIM : r - RIM + 8, part]).astype(
                        jnp.float32
                    )
                else:
                    depth = inside(rows_n[slot, :, part])
                for k in range(levels):
                    WET[k, j, r : r + 8, :] = (depth > k + 0.5).astype(jnp.float32)
                    BOT[k, j, r : r + 8, :] = jnp.where(jnp.abs(depth - (k + 1)) < 0.5, 1.0, 0.0)
            depth = inside(
                jnp.where(
                    flat_lane < 64,
                    strips[0, r : r + 8, 3 * LANES : 4 * LANES],
                    strips[1, r : r + 8, 3 * LANES : 4 * LANES],
                )
            )
            for k in range(levels):
                WET[k, tiles - 1, r : r + 8, :] = (depth > k + 0.5).astype(jnp.float32)
                BOT[k, tiles - 1, r : r + 8, :] = jnp.where(jnp.abs(depth - (k + 1)) < 0.5, 1.0, 0.0)
        else:
            for k in range(levels):
                WET[k, :, r : r + 8, :] = jnp.zeros((tiles, 8, LANES), jnp.float32)
        for p in range(planes):
            k = p % levels
            for j in range(tiles - 1):
                part = slice(j * LANES, (j + 1) * LANES)
                if own:
                    S[p, j, r : r + 8, :] = state[p, r - RIM : r - RIM + 8, part]
                    G[p, j, r : r + 8, :] = WET[k, j, r : r + 8, :] * cot[p, r - RIM : r - RIM + 8, part]
                else:
                    base = r if slot == 0 else r - rows - RIM
                    S[p, j, r : r + 8, :] = inside(rows_s[slot, p, base : base + 8, part])
                    if near:
                        G[p, j, r : r + 8, :] = WET[k, j, r : r + 8, :] * inside(rows_c[slot, p, :, part])
            half = p // 8
            S[p, tiles - 1, r : r + 8, :] = inside(
                third(slice(half * LANES, (half + 1) * LANES), 16, p % 8)
            )
            if near:
                G[p, tiles - 1, r : r + 8, :] = WET[k, tiles - 1, r : r + 8, :] * inside(
                    third(slice(2 * LANES, 3 * LANES), 8, p)
                )

    row = lax.broadcasted_iota(jnp.int32, (tall, LANES), 0) + (lat * rows - RIM)
    turn = jnp.pi * ((row.astype(jnp.float32) + 0.5) / (rows * lat_n) - 0.5)
    COR[...] = rotation * jnp.sin(turn)

    def sweep(first, count, body):
        def run(i, carry):
            body(first + 8 * i)
            return carry

        lax.fori_loop(0, count, run, 0)

    inner = rows // 8

    def open_faces(r):
        for k in range(levels):
            wet = at(WET, k, r)
            put(OX, k, r, wet * east(wet, 1) * (courant / 60.0))
            put(OY, k, r, wet * at(WET, k, r + 1) * (courant / 60.0))

    sweep(8, inner + 2, open_faces)

    def prepare(src, step):
        def body(r):
            press = None
            for k in range(levels):
                rho = at(WET, k, r) * (
                    (-0.2 * buoyancy) * at(src, k, r) + (0.8 * buoyancy) * at(src, levels + k, r)
                )
                press = rho if press is None else press + rho
                put(PR, k, r, press)
                u = at(src, 2 * levels + k, r)
                w = 0.5 * (u + east(u, 1))
                put(W, (step * 6) * levels + k, r, w)
                square = w * w + 0.0001
                root = lax.rsqrt(square)
                put(W, (step * 6 + 1) * levels + k, r, square * root)
                put(W, (step * 6 + 2) * levels + k, r, w * root)
                w = 0.5 * (at(src, 3 * levels + k, r) + at(src, 3 * levels + k, r + 1))
                put(W, (step * 6 + 3) * levels + k, r, w)
                square = w * w + 0.0001
                root = lax.rsqrt(square)
                put(W, (step * 6 + 4) * levels + k, r, square * root)
                put(W, (step * 6 + 5) * levels + k, r, w * root)

        sweep(8, inner + 2, body)

    bands = (inner + 2) // 2
    height = 16 * bands

    def split(target, p, i, column, v):
        high = v.astype(jnp.bfloat16)
        low = (v - high.astype(jnp.float32)).astype(jnp.bfloat16)
        width = tiles * LANES
        for start, part in ((column, high), (column + width, low)):
            target[p, 16 * i : 16 * i + 16, start : start + LANES] = part

    def lon_stencils(src):
        def part(p, carry):
            for j in range(tiles):
                for i in range(bands):
                    split(QB, p, i, j * LANES, src[p, j, 8 + 16 * i : 24 + 16 * i, :])
            return carry

        lax.fori_loop(0, planes, part, 0)
        left = QB[...].reshape(planes * height, 2 * tiles * LANES)
        for t in range(tiles):
            got = jnp.dot(
                left, ahead[:, 2 * t * LANES : 2 * (t + 1) * LANES], preferred_element_type=jnp.float32
            )
            for half in range(2):
                CD[:, 2 * t + half, 8 : 8 + height, :] = got[:, half * LANES : (half + 1) * LANES].reshape(
                    planes, height, LANES
                )

    def lon_transposed(grad, step):
        def part(k, carry):
            for i in range(bands):
                rows_i = slice(8 + 16 * i, 24 + 16 * i)
                base = step * 6
                ox = OX[k, :, rows_i, :]
                wx = W[base * levels + k, :, rows_i, :]
                sx = W[(base + 1) * levels + k, :, rows_i, :]
                by_speed = None
                for f in range(4):
                    p = f * levels + k
                    g = grad[p, :, rows_i, :]
                    h = ox * (east(g, 1) - g)
                    term = h * KX[step * planes + p, :, rows_i, :]
                    by_speed = term if by_speed is None else by_speed + term
                    zw = wx * h
                    zs = sx * h
                    for j in range(tiles):
                        split(ZB, p, i, j * LANES, zw[j])
                        split(ZB, p, i, (2 * tiles + j) * LANES, zs[j])
                LWX[k, :, rows_i, :] = 0.5 * (by_speed + east(by_speed, -1))
            return carry

        lax.fori_loop(0, levels, part, 0)
        left = ZB[...].reshape(planes * height, 4 * tiles * LANES)
        for t in range(0, tiles, 2):
            stop = min(t + 2, tiles)
            got = jnp.dot(left, behind[:, t * LANES : stop * LANES], preferred_element_type=jnp.float32)
            for j in range(t, stop):
                LX[:, j, 8 : 8 + height, :] = got[:, (j - t) * LANES : (j - t + 1) * LANES].reshape(
                    planes, height, LANES
                )

    def speeds(step, k, r, along):
        base = step * 6 + 3 * along
        return [at(W, (base + i) * levels + k, r) for i in range(3)]

    def stencil(c0, c1, c2, c3, c4, c5):
        central = 37.0 * (c2 + c3) - 8.0 * (c1 + c4) + (c0 + c5)
        damping = 10.0 * (c3 - c2) - 5.0 * (c4 - c1) + (c5 - c0)
        return central, damping

    def forward(src, dst, step, first, count):
        prepare(src, step)
        lon_stencils(src)

        def body(r):
            turn = COR[pl.ds(r, 8), :][None]

            def level(k, carry):
                wet = at(WET, k, r)
                ox = at(OX, k, r)
                oy = at(OY, k, r)
                wx, sx, tx = speeds(step, k, r, 0)
                wy, sy, ty = speeds(step, k, r, 1)
                lo = jnp.maximum(k - 1, 0)
                hi = jnp.minimum(k + 1, levels - 1)
                mix_lo = vert_mix * at(WET, lo, r)
                mix_hi = vert_mix * at(WET, hi, r)
                for f in range(4):
                    p = f * levels + k
                    q = at(src, p, r)
                    c = CD[p, :tiles, pl.ds(r, 8), :]
                    d = CD[p, tiles:, pl.ds(r, 8), :]
                    put(KX, step * planes + p, r, c - tx * d)
                    flux = ox * (wx * c - sx * d)
                    total = q - (flux - east(flux, -1))
                    c, d = stencil(*[at(src, p, r + o) for o in (-2, -1)], q, *[at(src, p, r + o) for o in (1, 2, 3)])
                    put(KY, step * planes + p, r, c - ty * d)
                    flux = oy * (wy * c - sy * d)
                    put(FA, p, r, flux)
                    total = total - (flux - at(FA, p, r - 1))
                    total = total + mix_lo * (at(src, f * levels + lo, r) - q)
                    total = total + mix_hi * (at(src, f * levels + hi, r) - q)
                    if f == 2:
                        press = at(PR, k, r)
                        total = total + turn * at(src, 3 * levels + k, r)
                        total = total - 0.5 * (east(press, 1) - east(press, -1))
                        total = total - bottom_drag * at(BOT, k, r) * q
                    if f == 3:
                        total = total - turn * at(src, 2 * levels + k, r)
                        total = total - 0.5 * (at(PR, k, r + 1) - at(PR, k, r - 1))
                        total = total - bottom_drag * at(BOT, k, r) * q
                    put(dst, p, r, wet * total)
                return carry

            lax.fori_loop(0, levels, level, 0)

        sweep(first, count, body)

    def backward(grad, step, first_face, faces, first, count, store):
        def face_body(r):
            def level(k, carry):
                oy = at(OY, k, r)
                wy, sy, _ = speeds(step, k, r, 1)
                by_speed = None
                for f in range(4):
                    p = f * levels + k
                    h = oy * (at(grad, p, r + 1) - at(grad, p, r))
                    put(FA, p, r, wy * h)
                    put(FB, p, r, sy * h)
                    term = h * at(KY, step * planes + p, r)
                    by_speed = term if by_speed is None else by_speed + term
                put(LWY, k, r, by_speed)
                return carry

            lax.fori_loop(0, levels, level, 0)

        sweep(first_face, faces, face_body)
        lon_transposed(grad, step)

        def body(r):
            turn = COR[pl.ds(r, 8), :][None]

            def level(i, below):
                k = levels - 1 - i
                wet = at(WET, k, r)
                lo = jnp.maximum(k - 1, 0)
                hi = jnp.minimum(k + 1, levels - 1)
                mix_wet = vert_mix * wet
                wet_lo = jnp.where(k > 0, 1.0, 0.0) * vert_mix * at(WET, lo, r)
                wet_hi = jnp.where(k < levels - 1, 1.0, 0.0) * vert_mix * at(WET, hi, r)
                has_lo = jnp.where(k > 0, 1.0, 0.0) * mix_wet
                has_hi = jnp.where(k < levels - 1, 1.0, 0.0) * mix_wet
                keep = 1.0 - wet_lo - wet_hi
                gu = at(grad, 2 * levels + k, r)
                gv = at(grad, 3 * levels + k, r)
                by_press = 0.5 * (east(gu, 1) - east(gu, -1)) + 0.5 * (
                    at(grad, 3 * levels + k, r + 1) - at(grad, 3 * levels + k, r - 1)
                )
                below = below + by_press
                by_rho = buoyancy * wet * below
                drag = bottom_drag * at(BOT, k, r)
                sums = []
                for f in range(4):
                    p = f * levels + k
                    g = at(grad, p, r)
                    total = keep * g + has_lo * at(grad, f * levels + lo, r) + has_hi * at(grad, f * levels + hi, r)
                    total = total + at(LX, p, r)
                    z = [at(FA, p, r + o) for o in range(-3, 3)]
                    total = total + (37.0 * (z[2] + z[3]) - 8.0 * (z[1] + z[4]) + (z[0] + z[5]))
                    z = [at(FB, p, r + o) for o in range(-3, 3)]
                    total = total + (10.0 * (z[3] - z[2]) - 5.0 * (z[4] - z[1]) + (z[5] - z[0]))
                    sums.append(total)
                speed_y = at(LWY, k, r) + at(LWY, k, r - 1)
                sums[0] = sums[0] - 0.2 * by_rho
                sums[1] = sums[1] + 0.8 * by_rho
                sums[2] = sums[2] + at(LWX, k, r) - turn * gv - drag * gu
                sums[3] = sums[3] + 0.5 * speed_y + turn * gu - drag * gv
                for f in range(4):
                    store(f * levels + k, r, sums[f], wet)
                return below

            lax.fori_loop(0, levels, level, jnp.zeros((tiles, 8, LANES), jnp.float32))

        sweep(first, count, body)

    forward(S, X1, 0, 8, inner + 2)
    forward(X1, X2, 1, RIM - 4, inner + 1)

    def store_middle(p, r, v, wet):
        put(A1, p, r, wet * v)

    def store_last(p, r, v, wet):
        row = pl.multiple_of(r - RIM, 8)
        for j in range(tiles - 1):
            adjoint[p, pl.ds(row, 8), j * LANES : (j + 1) * LANES] = v[j]

    backward(G, 1, 8, inner + 2, RIM - 4, inner + 1, store_middle)
    backward(A1, 0, RIM - 4, inner + 1, RIM, inner, store_last)
    for p in range(planes):
        for j in range(tiles - 1):
            final[p, :, j * LANES : (j + 1) * LANES] = X2[p, j, RIM : RIM + rows, :]


def band_matrices(width):
    central = np.zeros((width, width), np.float32)
    damping = np.zeros((width, width), np.float32)
    face = np.arange(width)
    for offset, c, d in ((-2, 1, -1), (-1, -8, 5), (0, 37, -10), (1, 37, 10), (2, -8, -5), (3, 1, 1)):
        central[(face + offset) % width, face] = c
        damping[(face + offset) % width, face] = d
    both = np.concatenate([central, damping], axis=1)
    ahead = np.concatenate([both, both], axis=0)
    behind = np.concatenate([central.T, central.T, -damping.T, -damping.T], axis=0)
    return jnp.asarray(ahead, jnp.bfloat16), jnp.asarray(behind, jnp.bfloat16)


def steps(lat_n, state, cot, sea, lev, halos):
    planes, rows, cols = state.shape
    levels = planes // 4
    f32 = jnp.float32
    tall = rows + 2 * RIM
    tiles = cols // LANES + 1

    def scratch(count):
        return pltpu.VMEM((count, tiles, tall, LANES), f32)

    width = tiles * LANES
    height = rows + 16
    shapes = [scratch(count) for count in [planes] * 8 + [2 * planes] * 2]
    shapes.append(pltpu.VMEM((planes, 2 * tiles, tall, LANES), f32))
    shapes += [scratch(count) for count in [levels] * 5 + [12 * levels, levels, levels]]
    shapes.append(pltpu.VMEM((tall, LANES), f32))
    shapes.append(pltpu.VMEM((planes, height, 2 * width), jnp.bfloat16))
    shapes.append(pltpu.VMEM((planes, height, 4 * width), jnp.bfloat16))
    return pl.pallas_call(
        functools.partial(step_kernel, lat_n),
        out_shape=(jax.ShapeDtypeStruct(state.shape, f32),) * 2,
        in_specs=[pl.BlockSpec(memory_space=pltpu.VMEM)] * 10,
        out_specs=(pl.BlockSpec(memory_space=pltpu.VMEM),) * 2,
        scratch_shapes=shapes,
        compiler_params=pltpu.CompilerParams(vmem_limit_bytes=56 * 1024 * 1024),
        name="steps",
    )(state, cot, sea, lev, *halos, *band_matrices(width))


def shards(state, cotangent, seamask, levels):
    shape = state.shape
    flat = (shape[0] * shape[1], shape[2], shape[3])
    state = state.reshape(flat)
    cotangent = cotangent.reshape(flat)
    halos = exchange(state, cotangent, seamask, levels)
    final, adjoint = steps(lax.axis_size("lat"), state, cotangent, seamask, levels, halos)
    return (final.reshape(shape), adjoint.reshape(shape))


def solution(mesh):
    placed = (
        P(None, None, "lat", "lon"),
        P(None, None, "lat", "lon"),
        P("lat", "lon"),
        P("lat", "lon"),
    )
    return jax.shard_map(
        shards,
        mesh=mesh,
        in_specs=placed,
        out_specs=(P(None, None, "lat", "lon"), P(None, None, "lat", "lon")),
        check_vma=False,
    )
```

```python
import functools

import jax
import jax.numpy as jnp
import numpy as np
from jax import lax
from jax.experimental import pallas as pl
from jax.experimental.pallas import tpu as pltpu
from jax.sharding import PartitionSpec as P

courant = 0.4
vert_mix = 0.1
rotation = 0.3
buoyancy = 0.3
bottom_drag = 0.2

LANES = 128
RIM = 16
MESH = pl.DeviceIdType.MESH


def exchange_kernel(
    state, cot, sea, lev, rows_s, rows_9, rows_c, rows_n, strips, pack, ninth, depth, send, recv
):
    planes, rows, cols = state.shape
    lon = lax.axis_index("lon")
    lat = lax.axis_index("lat")
    lon_n = lax.axis_size("lon")
    lat_n = lax.axis_size("lat")
    left = lax.rem(lon + lon_n - 1, lon_n)
    right = lax.rem(lon + 1, lon_n)
    has_up = lat > 0
    has_down = lat < lat_n - 1

    barrier = pltpu.get_barrier_semaphore()

    def greet(to_lon, to_lat):
        pl.semaphore_signal(barrier, inc=1, device_id=(to_lon, to_lat), device_id_type=MESH)

    greet(left, lat)
    greet(right, lat)

    @pl.when(has_up)
    def _():
        for to_lon in (left, lon, right):
            greet(to_lon, lat - 1)

    @pl.when(has_down)
    def _():
        for to_lon in (left, lon, right):
            greet(to_lon, lat + 1)

    depth[...] = (sea[...] * lev[...]).astype(jnp.float32)
    ninth[0] = state[:, 8, :]
    ninth[1] = state[:, rows - 9, :]
    sides = jnp.where(has_up, 1, 0) + jnp.where(has_down, 1, 0)
    pl.semaphore_wait(barrier, 2 + 3 * sides)

    def message(number, source, target, to_lon, to_lat):
        return pltpu.make_async_remote_copy(
            src_ref=source,
            dst_ref=target,
            send_sem=send.at[number],
            recv_sem=recv.at[number],
            device_id=(to_lon, to_lat),
            device_id_type=MESH,
        )

    end = rows + RIM
    sideways = [
        message(0, pack.at[0], strips.at[0, RIM:end], left, lat),
        message(1, pack.at[1], strips.at[1, RIM:end], right, lat),
    ]
    up_rows = [
        message(2, state.at[:, 0:8], rows_s.at[1], lon, lat - 1),
        message(12, ninth.at[0], rows_9.at[1], lon, lat - 1),
        message(3, cot.at[:, 0:8], rows_c.at[1], lon, lat - 1),
        message(4, depth.at[0:8], rows_n.at[1], lon, lat - 1),
    ]
    up_strips = [
        message(5, pack.at[0, 0:RIM], strips.at[0, end : end + RIM], left, lat - 1),
        message(6, pack.at[1, 0:RIM], strips.at[1, end : end + RIM], right, lat - 1),
    ]
    down_rows = [
        message(7, state.at[:, rows - 8 : rows], rows_s.at[0], lon, lat + 1),
        message(13, ninth.at[1], rows_9.at[0], lon, lat + 1),
        message(8, cot.at[:, rows - 8 : rows], rows_c.at[0], lon, lat + 1),
        message(9, depth.at[rows - 8 : rows], rows_n.at[0], lon, lat + 1),
    ]
    down_strips = [
        message(10, pack.at[0, rows - RIM : rows], strips.at[0, 0:RIM], left, lat + 1),
        message(11, pack.at[1, rows - RIM : rows], strips.at[1, 0:RIM], right, lat + 1),
    ]

    up = up_rows + up_strips
    down = down_rows + down_strips

    @pl.when(has_up)
    def _():
        for copy in up_rows:
            copy.start()

    @pl.when(has_down)
    def _():
        for copy in down_rows:
            copy.start()

    lane = lax.broadcasted_iota(jnp.int32, (rows, LANES), 1)
    for side in range(2):
        part = slice(0, LANES) if side == 0 else slice(cols - LANES, cols)
        for half in range(2):
            total = jnp.zeros((rows, LANES), jnp.float32)
            for slot in range(8):
                origin = 0 if side == 0 else LANES - 16
                moved = pltpu.roll(state[half * 8 + slot, :, part], (16 * slot - origin) % LANES, 1)
                total = jnp.where(lane // 16 == slot, moved, total)
            pack[side, :, half * LANES : (half + 1) * LANES] = total
        total = jnp.zeros((rows, LANES), jnp.float32)
        for slot in range(16):
            origin = 0 if side == 0 else LANES - 8
            moved = pltpu.roll(cot[slot, :, part], (8 * slot - origin) % LANES, 1)
            total = jnp.where(lane // 8 == slot, moved, total)
        pack[side, :, 2 * LANES : 3 * LANES] = total
        pack[side, :, 3 * LANES : 4 * LANES] = depth[:, part]

    for copy in sideways:
        copy.start()

    @pl.when(has_up)
    def _():
        for copy in up_strips:
            copy.start()

    @pl.when(has_down)
    def _():
        for copy in down_strips:
            copy.start()

    for copy in sideways:
        copy.wait()

    @pl.when(has_up)
    def _():
        for copy in up:
            copy.wait_send()
        for copy in down:
            copy.wait_recv()

    @pl.when(has_down)
    def _():
        for copy in down:
            copy.wait_send()
        for copy in up:
            copy.wait_recv()


def exchange(state, cot, sea, lev):
    planes, rows, cols = state.shape
    f32 = jnp.float32
    return pl.pallas_call(
        exchange_kernel,
        out_shape=(
            jax.ShapeDtypeStruct((2, planes, 8, cols), f32),
            jax.ShapeDtypeStruct((2, planes, cols), f32),
            jax.ShapeDtypeStruct((2, planes, 8, cols), f32),
            jax.ShapeDtypeStruct((2, 8, cols), f32),
            jax.ShapeDtypeStruct((2, rows + 2 * RIM, 4 * LANES), f32),
        ),
        in_specs=[pl.BlockSpec(memory_space=pltpu.VMEM)] * 4,
        out_specs=[pl.BlockSpec(memory_space=pl.ANY)] * 5,
        scratch_shapes=[
            pltpu.VMEM((2, rows, 4 * LANES), f32),
            pltpu.VMEM((2, planes, cols), f32),
            pltpu.VMEM((rows, cols), f32),
            pltpu.SemaphoreType.DMA((14,)),
            pltpu.SemaphoreType.DMA((14,)),
        ],
        compiler_params=pltpu.CompilerParams(collective_id=0, has_side_effects=True),
        name="exchange",
    )(state, cot, sea, lev)


def step_kernel(
    lat_n, state, cot, sea, lev, rows_s, rows_9, rows_c, rows_n, strips, ahead, behind, final, adjoint,
    S, G, X1, X2, A1, FA, FB, LX, KX, KY, CD, WET, BOT, OX, OY, PR, W, LWY, LWX, COR, QB, ZB,
):
    planes, rows, cols = state.shape
    levels = WET.shape[0]
    tall = rows + 2 * RIM
    tiles = cols // LANES + 1
    lat = lax.axis_index("lat")
    lanes = {n: lax.broadcasted_iota(jnp.int32, (tiles, n, LANES), 2) for n in (8, 16)}
    flat_lane = lax.broadcasted_iota(jnp.int32, (8, LANES), 1)
    lat_vec = jnp.full((8, LANES), lat, jnp.int32)

    def east(v, d):
        lane = lanes[v.shape[1]]
        rolled = pltpu.roll(v, (-d) % LANES, 2)
        if d > 0:
            other = jnp.concatenate([rolled[1:], rolled[:1]], axis=0)
            return jnp.where(lane < LANES - d, rolled, other)
        other = jnp.concatenate([rolled[-1:], rolled[:-1]], axis=0)
        return jnp.where(lane >= -d, rolled, other)

    def at(ref, p, r):
        return ref[p, :, pl.ds(r, 8), :]

    def put(ref, p, r, v):
        ref[p, :, pl.ds(r, 8), :] = v

    for t in range(tall // 8):
        r = 8 * t
        own = RIM <= r < rows + RIM
        slot = 0 if r < RIM else 1
        edge = (lat_vec > 0) if r < RIM else (lat_vec < lat_n - 1)

        def inside(v):
            return v if own else jnp.where(edge, v, 0.0)

        def third(tile, width, place):
            right = pltpu.roll(strips[0, r : r + 8, tile], (-width * place) % LANES, 1)
            if width * place == 0:
                right = strips[0, r : r + 8, tile]
            shift = (LANES - width - width * place) % LANES
            left = strips[1, r : r + 8, tile]
            if shift:
                left = pltpu.roll(left, shift, 1)
            return jnp.where(flat_lane < 64, right, left)

        near = RIM - 8 <= r < rows + RIM + 8
        if near:
            for j in range(tiles - 1):
                part = slice(j * LANES, (j + 1) * LANES)
                if own:
                    depth = (sea[r - RIM : r - RIM + 8, part] * lev[r - RIM : r - RIM + 8, part]).astype(
                        jnp.float32
                    )
                else:
                    depth = inside(rows_n[slot, :, part])
                for k in range(levels):
                    WET[k, j, r : r + 8, :] = (depth > k + 0.5).astype(jnp.float32)
                    BOT[k, j, r : r + 8, :] = jnp.where(jnp.abs(depth - (k + 1)) < 0.5, 1.0, 0.0)
            depth = inside(
                jnp.where(
                    flat_lane < 64,
                    strips[0, r : r + 8, 3 * LANES : 4 * LANES],
                    strips[1, r : r + 8, 3 * LANES : 4 * LANES],
                )
            )
            for k in range(levels):
                WET[k, tiles - 1, r : r + 8, :] = (depth > k + 0.5).astype(jnp.float32)
                BOT[k, tiles - 1, r : r + 8, :] = jnp.where(jnp.abs(depth - (k + 1)) < 0.5, 1.0, 0.0)
        else:
            for k in range(levels):
                WET[k, :, r : r + 8, :] = jnp.zeros((tiles, 8, LANES), jnp.float32)
        for p in range(planes):
            k = p % levels
            for j in range(tiles - 1):
                part = slice(j * LANES, (j + 1) * LANES)
                if own:
                    S[p, j, r : r + 8, :] = state[p, r - RIM : r - RIM + 8, part]
                    G[p, j, r : r + 8, :] = WET[k, j, r : r + 8, :] * cot[p, r - RIM : r - RIM + 8, part]
                else:
                    if near:
                        S[p, j, r : r + 8, :] = inside(rows_s[slot, p, :, part])
                        G[p, j, r : r + 8, :] = WET[k, j, r : r + 8, :] * inside(rows_c[slot, p, :, part])
                    else:
                        outer = jnp.broadcast_to(rows_9[slot, p : p + 1, part], (8, LANES))
                        S[p, j, r : r + 8, :] = inside(outer)
            half = p // 8
            S[p, tiles - 1, r : r + 8, :] = inside(
                third(slice(half * LANES, (half + 1) * LANES), 16, p % 8)
            )
            if near:
                G[p, tiles - 1, r : r + 8, :] = WET[k, tiles - 1, r : r + 8, :] * inside(
                    third(slice(2 * LANES, 3 * LANES), 8, p)
                )

    row = lax.broadcasted_iota(jnp.int32, (tall, LANES), 0) + (lat * rows - RIM)
    turn = jnp.pi * ((row.astype(jnp.float32) + 0.5) / (rows * lat_n) - 0.5)
    COR[...] = rotation * jnp.sin(turn)

    def sweep(first, count, body):
        def run(i, carry):
            body(first + 8 * i)
            return carry

        lax.fori_loop(0, count, run, 0)

    inner = rows // 8

    def open_faces(r):
        for k in range(levels):
            wet = at(WET, k, r)
            put(OX, k, r, wet * east(wet, 1) * (courant / 60.0))
            put(OY, k, r, wet * at(WET, k, r + 1) * (courant / 60.0))

    sweep(8, inner + 2, open_faces)

    def prepare(src, step):
        def body(r):
            press = None
            for k in range(levels):
                rho = at(WET, k, r) * (
                    (-0.2 * buoyancy) * at(src, k, r) + (0.8 * buoyancy) * at(src, levels + k, r)
                )
                press = rho if press is None else press + rho
                put(PR, k, r, press)
                u = at(src, 2 * levels + k, r)
                w = 0.5 * (u + east(u, 1))
                put(W, (step * 6) * levels + k, r, w)
                square = w * w + 0.0001
                root = lax.rsqrt(square)
                put(W, (step * 6 + 1) * levels + k, r, square * root)
                put(W, (step * 6 + 2) * levels + k, r, w * root)
                w = 0.5 * (at(src, 3 * levels + k, r) + at(src, 3 * levels + k, r + 1))
                put(W, (step * 6 + 3) * levels + k, r, w)
                square = w * w + 0.0001
                root = lax.rsqrt(square)
                put(W, (step * 6 + 4) * levels + k, r, square * root)
                put(W, (step * 6 + 5) * levels + k, r, w * root)

        sweep(8, inner + 2, body)

    bands = (inner + 2) // 2
    height = 16 * bands

    def split(target, p, i, column, v):
        high = v.astype(jnp.bfloat16)
        low = (v - high.astype(jnp.float32)).astype(jnp.bfloat16)
        width = tiles * LANES
        for start, part in ((column, high), (column + width, low)):
            target[p, 16 * i : 16 * i + 16, start : start + LANES] = part

    def lon_stencils(src):
        def part(p, carry):
            for j in range(tiles):
                for i in range(bands):
                    split(QB, p, i, j * LANES, src[p, j, 8 + 16 * i : 24 + 16 * i, :])
            return carry

        lax.fori_loop(0, planes, part, 0)
        left = QB[...].reshape(planes * height, 2 * tiles * LANES)
        for t in range(tiles):
            got = jnp.dot(
                left, ahead[:, 2 * t * LANES : 2 * (t + 1) * LANES], preferred_element_type=jnp.float32
            )
            for half in range(2):
                CD[:, 2 * t + half, 8 : 8 + height, :] = got[:, half * LANES : (half + 1) * LANES].reshape(
                    planes, height, LANES
                )

    def lon_transposed(grad, step):
        def part(k, carry):
            for i in range(bands):
                rows_i = slice(8 + 16 * i, 24 + 16 * i)
                base = step * 6
                ox = OX[k, :, rows_i, :]
                wx = W[base * levels + k, :, rows_i, :]
                sx = W[(base + 1) * levels + k, :, rows_i, :]
                by_speed = None
                for f in range(4):
                    p = f * levels + k
                    g = grad[p, :, rows_i, :]
                    h = ox * (east(g, 1) - g)
                    term = h * KX[step * planes + p, :, rows_i, :]
                    by_speed = term if by_speed is None else by_speed + term
                    zw = wx * h
                    zs = sx * h
                    for j in range(tiles):
                        split(ZB, p, i, j * LANES, zw[j])
                        split(ZB, p, i, (2 * tiles + j) * LANES, zs[j])
                LWX[k, :, rows_i, :] = 0.5 * (by_speed + east(by_speed, -1))
            return carry

        lax.fori_loop(0, levels, part, 0)
        left = ZB[...].reshape(planes * height, 4 * tiles * LANES)
        for t in range(0, tiles, 2):
            stop = min(t + 2, tiles)
            got = jnp.dot(left, behind[:, t * LANES : stop * LANES], preferred_element_type=jnp.float32)
            for j in range(t, stop):
                LX[:, j, 8 : 8 + height, :] = got[:, (j - t) * LANES : (j - t + 1) * LANES].reshape(
                    planes, height, LANES
                )

    def speeds(step, k, r, along):
        base = step * 6 + 3 * along
        return [at(W, (base + i) * levels + k, r) for i in range(3)]

    def stencil(c0, c1, c2, c3, c4, c5):
        central = 37.0 * (c2 + c3) - 8.0 * (c1 + c4) + (c0 + c5)
        damping = 10.0 * (c3 - c2) - 5.0 * (c4 - c1) + (c5 - c0)
        return central, damping

    def forward(src, dst, step, first, count):
        prepare(src, step)
        lon_stencils(src)

        def body(r):
            turn = COR[pl.ds(r, 8), :][None]

            def level(k, carry):
                wet = at(WET, k, r)
                ox = at(OX, k, r)
                oy = at(OY, k, r)
                wx, sx, tx = speeds(step, k, r, 0)
                wy, sy, ty = speeds(step, k, r, 1)
                lo = jnp.maximum(k - 1, 0)
                hi = jnp.minimum(k + 1, levels - 1)
                mix_lo = vert_mix * at(WET, lo, r)
                mix_hi = vert_mix * at(WET, hi, r)
                for f in range(4):
                    p = f * levels + k
                    q = at(src, p, r)
                    c = CD[p, :tiles, pl.ds(r, 8), :]
                    d = CD[p, tiles:, pl.ds(r, 8), :]
                    put(KX, step * planes + p, r, c - tx * d)
                    flux = ox * (wx * c - sx * d)
                    total = q - (flux - east(flux, -1))
                    c, d = stencil(*[at(src, p, r + o) for o in (-2, -1)], q, *[at(src, p, r + o) for o in (1, 2, 3)])
                    put(KY, step * planes + p, r, c - ty * d)
                    flux = oy * (wy * c - sy * d)
                    put(FA, p, r, flux)
                    total = total - (flux - at(FA, p, r - 1))
                    total = total + mix_lo * (at(src, f * levels + lo, r) - q)
                    total = total + mix_hi * (at(src, f * levels + hi, r) - q)
                    if f == 2:
                        press = at(PR, k, r)
                        total = total + turn * at(src, 3 * levels + k, r)
                        total = total - 0.5 * (east(press, 1) - east(press, -1))
                        total = total - bottom_drag * at(BOT, k, r) * q
                    if f == 3:
                        total = total - turn * at(src, 2 * levels + k, r)
                        total = total - 0.5 * (at(PR, k, r + 1) - at(PR, k, r - 1))
                        total = total - bottom_drag * at(BOT, k, r) * q
                    put(dst, p, r, wet * total)
                return carry

            lax.fori_loop(0, levels, level, 0)

        sweep(first, count, body)

    def backward(grad, step, first_face, faces, first, count, store):
        def face_body(r):
            def level(k, carry):
                oy = at(OY, k, r)
                wy, sy, _ = speeds(step, k, r, 1)
                by_speed = None
                for f in range(4):
                    p = f * levels + k
                    h = oy * (at(grad, p, r + 1) - at(grad, p, r))
                    put(FA, p, r, wy * h)
                    put(FB, p, r, sy * h)
                    term = h * at(KY, step * planes + p, r)
                    by_speed = term if by_speed is None else by_speed + term
                put(LWY, k, r, by_speed)
                return carry

            lax.fori_loop(0, levels, level, 0)

        sweep(first_face, faces, face_body)
        lon_transposed(grad, step)

        def body(r):
            turn = COR[pl.ds(r, 8), :][None]

            def level(i, below):
                k = levels - 1 - i
                wet = at(WET, k, r)
                lo = jnp.maximum(k - 1, 0)
                hi = jnp.minimum(k + 1, levels - 1)
                mix_wet = vert_mix * wet
                wet_lo = jnp.where(k > 0, 1.0, 0.0) * vert_mix * at(WET, lo, r)
                wet_hi = jnp.where(k < levels - 1, 1.0, 0.0) * vert_mix * at(WET, hi, r)
                has_lo = jnp.where(k > 0, 1.0, 0.0) * mix_wet
                has_hi = jnp.where(k < levels - 1, 1.0, 0.0) * mix_wet
                keep = 1.0 - wet_lo - wet_hi
                gu = at(grad, 2 * levels + k, r)
                gv = at(grad, 3 * levels + k, r)
                by_press = 0.5 * (east(gu, 1) - east(gu, -1)) + 0.5 * (
                    at(grad, 3 * levels + k, r + 1) - at(grad, 3 * levels + k, r - 1)
                )
                below = below + by_press
                by_rho = buoyancy * wet * below
                drag = bottom_drag * at(BOT, k, r)
                sums = []
                for f in range(4):
                    p = f * levels + k
                    g = at(grad, p, r)
                    total = keep * g + has_lo * at(grad, f * levels + lo, r) + has_hi * at(grad, f * levels + hi, r)
                    total = total + at(LX, p, r)
                    z = [at(FA, p, r + o) for o in range(-3, 3)]
                    total = total + (37.0 * (z[2] + z[3]) - 8.0 * (z[1] + z[4]) + (z[0] + z[5]))
                    z = [at(FB, p, r + o) for o in range(-3, 3)]
                    total = total + (10.0 * (z[3] - z[2]) - 5.0 * (z[4] - z[1]) + (z[5] - z[0]))
                    sums.append(total)
                speed_y = at(LWY, k, r) + at(LWY, k, r - 1)
                sums[0] = sums[0] - 0.2 * by_rho
                sums[1] = sums[1] + 0.8 * by_rho
                sums[2] = sums[2] + at(LWX, k, r) - turn * gv - drag * gu
                sums[3] = sums[3] + 0.5 * speed_y + turn * gu - drag * gv
                for f in range(4):
                    store(f * levels + k, r, sums[f], wet)
                return below

            lax.fori_loop(0, levels, level, jnp.zeros((tiles, 8, LANES), jnp.float32))

        sweep(first, count, body)

    forward(S, X1, 0, 8, inner + 2)
    forward(X1, X2, 1, RIM - 4, inner + 1)

    def store_middle(p, r, v, wet):
        put(A1, p, r, wet * v)

    def store_last(p, r, v, wet):
        row = pl.multiple_of(r - RIM, 8)
        for j in range(tiles - 1):
            adjoint[p, pl.ds(row, 8), j * LANES : (j + 1) * LANES] = v[j]

    backward(G, 1, 8, inner + 2, RIM - 4, inner + 1, store_middle)
    backward(A1, 0, RIM - 4, inner + 1, RIM, inner, store_last)
    for p in range(planes):
        for j in range(tiles - 1):
            final[p, :, j * LANES : (j + 1) * LANES] = X2[p, j, RIM : RIM + rows, :]


def band_matrices(width):
    central = np.zeros((width, width), np.float32)
    damping = np.zeros((width, width), np.float32)
    face = np.arange(width)
    for offset, c, d in ((-2, 1, -1), (-1, -8, 5), (0, 37, -10), (1, 37, 10), (2, -8, -5), (3, 1, 1)):
        central[(face + offset) % width, face] = c
        damping[(face + offset) % width, face] = d
    both = np.concatenate([central, damping], axis=1)
    ahead = np.concatenate([both, both], axis=0)
    behind = np.concatenate([central.T, central.T, -damping.T, -damping.T], axis=0)
    return jnp.asarray(ahead, jnp.bfloat16), jnp.asarray(behind, jnp.bfloat16)


def steps(lat_n, state, cot, sea, lev, halos):
    planes, rows, cols = state.shape
    levels = planes // 4
    f32 = jnp.float32
    tall = rows + 2 * RIM
    tiles = cols // LANES + 1

    def scratch(count):
        return pltpu.VMEM((count, tiles, tall, LANES), f32)

    width = tiles * LANES
    height = rows + 16
    shapes = [scratch(count) for count in [planes] * 8 + [2 * planes] * 2]
    shapes.append(pltpu.VMEM((planes, 2 * tiles, tall, LANES), f32))
    shapes += [scratch(count) for count in [levels] * 5 + [12 * levels, levels, levels]]
    shapes.append(pltpu.VMEM((tall, LANES), f32))
    shapes.append(pltpu.VMEM((planes, height, 2 * width), jnp.bfloat16))
    shapes.append(pltpu.VMEM((planes, height, 4 * width), jnp.bfloat16))
    return pl.pallas_call(
        functools.partial(step_kernel, lat_n),
        out_shape=(jax.ShapeDtypeStruct(state.shape, f32),) * 2,
        in_specs=[pl.BlockSpec(memory_space=pltpu.VMEM)] * 11,
        out_specs=(pl.BlockSpec(memory_space=pltpu.VMEM),) * 2,
        scratch_shapes=shapes,
        compiler_params=pltpu.CompilerParams(vmem_limit_bytes=56 * 1024 * 1024),
        name="steps",
    )(state, cot, sea, lev, *halos, *band_matrices(width))


def shards(state, cotangent, seamask, levels):
    shape = state.shape
    flat = (shape[0] * shape[1], shape[2], shape[3])
    state = state.reshape(flat)
    cotangent = cotangent.reshape(flat)
    halos = exchange(state, cotangent, seamask, levels)
    final, adjoint = steps(lax.axis_size("lat"), state, cotangent, seamask, levels, halos)
    return (final.reshape(shape), adjoint.reshape(shape))


def solution(mesh):
    placed = (
        P(None, None, "lat", "lon"),
        P(None, None, "lat", "lon"),
        P("lat", "lon"),
        P("lat", "lon"),
    )
    return jax.shard_map(
        shards,
        mesh=mesh,
        in_specs=placed,
        out_specs=(P(None, None, "lat", "lon"), P(None, None, "lat", "lon")),
        check_vma=False,
    )
```

```python
import functools

import jax
import jax.numpy as jnp
import numpy as np
from jax import lax
from jax.experimental import pallas as pl
from jax.experimental.pallas import tpu as pltpu
from jax.sharding import PartitionSpec as P

courant = 0.4
vert_mix = 0.1
rotation = 0.3
buoyancy = 0.3
bottom_drag = 0.2

LANES = 128
RIM = 16
MESH = pl.DeviceIdType.MESH


def exchange_kernel(
    state, cot, sea, lev, rows_s, rows_9, rows_c, rows_n, strips, pack, ninth, depth, send, recv
):
    planes, rows, cols = state.shape
    lon = lax.axis_index("lon")
    lat = lax.axis_index("lat")
    lon_n = lax.axis_size("lon")
    lat_n = lax.axis_size("lat")
    left = lax.rem(lon + lon_n - 1, lon_n)
    right = lax.rem(lon + 1, lon_n)
    has_up = lat > 0
    has_down = lat < lat_n - 1

    barrier = pltpu.get_barrier_semaphore()

    def greet(to_lon, to_lat):
        pl.semaphore_signal(barrier, inc=1, device_id=(to_lon, to_lat), device_id_type=MESH)

    greet(left, lat)
    greet(right, lat)

    @pl.when(has_up)
    def _():
        for to_lon in (left, lon, right):
            greet(to_lon, lat - 1)

    @pl.when(has_down)
    def _():
        for to_lon in (left, lon, right):
            greet(to_lon, lat + 1)

    depth[...] = (sea[...] * lev[...]).astype(jnp.float32)
    ninth[0] = state[:, 8, :]
    ninth[1] = state[:, rows - 9, :]
    sides = jnp.where(has_up, 1, 0) + jnp.where(has_down, 1, 0)
    pl.semaphore_wait(barrier, 2 + 3 * sides)

    def message(number, source, target, to_lon, to_lat):
        return pltpu.make_async_remote_copy(
            src_ref=source,
            dst_ref=target,
            send_sem=send.at[number],
            recv_sem=recv.at[number],
            device_id=(to_lon, to_lat),
            device_id_type=MESH,
        )

    end = rows + RIM
    sideways = [
        message(0, pack.at[0], strips.at[0, RIM:end], left, lat),
        message(1, pack.at[1], strips.at[1, RIM:end], right, lat),
    ]
    up_rows = [
        message(2, state.at[:, 0:8], rows_s.at[1], lon, lat - 1),
        message(12, ninth.at[0], rows_9.at[1], lon, lat - 1),
        message(3, cot.at[:, 0:8], rows_c.at[1], lon, lat - 1),
        message(4, depth.at[0:8], rows_n.at[1], lon, lat - 1),
    ]
    up_strips = [
        message(5, pack.at[0, 0:RIM], strips.at[0, end : end + RIM], left, lat - 1),
        message(6, pack.at[1, 0:RIM], strips.at[1, end : end + RIM], right, lat - 1),
    ]
    down_rows = [
        message(7, state.at[:, rows - 8 : rows], rows_s.at[0], lon, lat + 1),
        message(13, ninth.at[1], rows_9.at[0], lon, lat + 1),
        message(8, cot.at[:, rows - 8 : rows], rows_c.at[0], lon, lat + 1),
        message(9, depth.at[rows - 8 : rows], rows_n.at[0], lon, lat + 1),
    ]
    down_strips = [
        message(10, pack.at[0, rows - RIM : rows], strips.at[0, 0:RIM], left, lat + 1),
        message(11, pack.at[1, rows - RIM : rows], strips.at[1, 0:RIM], right, lat + 1),
    ]

    up = up_rows + up_strips
    down = down_rows + down_strips

    @pl.when(has_up)
    def _():
        for copy in up_rows:
            copy.start()

    @pl.when(has_down)
    def _():
        for copy in down_rows:
            copy.start()

    lane = lax.broadcasted_iota(jnp.int32, (rows, LANES), 1)
    for side in range(2):
        part = slice(0, LANES) if side == 0 else slice(cols - LANES, cols)
        for half in range(2):
            total = jnp.zeros((rows, LANES), jnp.float32)
            for slot in range(8):
                origin = 0 if side == 0 else LANES - 16
                moved = pltpu.roll(state[half * 8 + slot, :, part], (16 * slot - origin) % LANES, 1)
                total = jnp.where(lane // 16 == slot, moved, total)
            pack[side, :, half * LANES : (half + 1) * LANES] = total
        total = jnp.zeros((rows, LANES), jnp.float32)
        for slot in range(16):
            origin = 0 if side == 0 else LANES - 8
            moved = pltpu.roll(cot[slot, :, part], (8 * slot - origin) % LANES, 1)
            total = jnp.where(lane // 8 == slot, moved, total)
        pack[side, :, 2 * LANES : 3 * LANES] = total
        pack[side, :, 3 * LANES : 4 * LANES] = depth[:, part]

    for copy in sideways:
        copy.start()

    @pl.when(has_up)
    def _():
        for copy in up_strips:
            copy.start()

    @pl.when(has_down)
    def _():
        for copy in down_strips:
            copy.start()

    for copy in sideways:
        copy.wait()

    @pl.when(has_up)
    def _():
        for copy in up:
            copy.wait_send()
        for copy in down:
            copy.wait_recv()

    @pl.when(has_down)
    def _():
        for copy in down:
            copy.wait_send()
        for copy in up:
            copy.wait_recv()


def exchange(state, cot, sea, lev):
    planes, rows, cols = state.shape
    f32 = jnp.float32
    return pl.pallas_call(
        exchange_kernel,
        out_shape=(
            jax.ShapeDtypeStruct((2, planes, 8, cols), f32),
            jax.ShapeDtypeStruct((2, planes, cols), f32),
            jax.ShapeDtypeStruct((2, planes, 8, cols), f32),
            jax.ShapeDtypeStruct((2, 8, cols), f32),
            jax.ShapeDtypeStruct((2, rows + 2 * RIM, 4 * LANES), f32),
        ),
        in_specs=[pl.BlockSpec(memory_space=pltpu.VMEM)] * 4,
        out_specs=[pl.BlockSpec(memory_space=pl.ANY)] * 5,
        scratch_shapes=[
            pltpu.VMEM((2, rows, 4 * LANES), f32),
            pltpu.VMEM((2, planes, cols), f32),
            pltpu.VMEM((rows, cols), f32),
            pltpu.SemaphoreType.DMA((14,)),
            pltpu.SemaphoreType.DMA((14,)),
        ],
        compiler_params=pltpu.CompilerParams(collective_id=0, has_side_effects=True),
        name="exchange",
    )(state, cot, sea, lev)


def step_kernel(
    lat_n, state, cot, sea, lev, rows_s, rows_9, rows_c, rows_n, strips, ahead, behind, final, adjoint,
    S, G, X1, X2, A1, FA, FB, LX, KX, KY, CD, WET, BOT, OX, OY, PR, W, LWY, LWX, COR, QB, ZB,
):
    planes, rows, cols = state.shape
    levels = WET.shape[0]
    tall = rows + 2 * RIM
    tiles = cols // LANES + 1
    lat = lax.axis_index("lat")
    lanes = {n: lax.broadcasted_iota(jnp.int32, (tiles, n, LANES), 2) for n in (8, 16)}
    flat_lane = lax.broadcasted_iota(jnp.int32, (8, LANES), 1)
    lat_vec = jnp.full((8, LANES), lat, jnp.int32)

    def east(v, d):
        lane = lanes[v.shape[1]]
        rolled = pltpu.roll(v, (-d) % LANES, 2)
        if d > 0:
            other = jnp.concatenate([rolled[1:], rolled[:1]], axis=0)
            return jnp.where(lane < LANES - d, rolled, other)
        other = jnp.concatenate([rolled[-1:], rolled[:-1]], axis=0)
        return jnp.where(lane >= -d, rolled, other)

    def at(ref, p, r):
        return ref[p, :, pl.ds(r, 8), :]

    def put(ref, p, r, v):
        ref[p, :, pl.ds(r, 8), :] = v

    for t in range(tall // 8):
        r = 8 * t
        own = RIM <= r < rows + RIM
        slot = 0 if r < RIM else 1
        edge = (lat_vec > 0) if r < RIM else (lat_vec < lat_n - 1)

        def inside(v):
            return v if own else jnp.where(edge, v, 0.0)

        def third(tile, width, place):
            right = pltpu.roll(strips[0, r : r + 8, tile], (-width * place) % LANES, 1)
            if width * place == 0:
                right = strips[0, r : r + 8, tile]
            shift = (LANES - width - width * place) % LANES
            left = strips[1, r : r + 8, tile]
            if shift:
                left = pltpu.roll(left, shift, 1)
            return jnp.where(flat_lane < 64, right, left)

        near = RIM - 8 <= r < rows + RIM + 8
        if near:
            for j in range(tiles - 1):
                part = slice(j * LANES, (j + 1) * LANES)
                if own:
                    depth = (sea[r - RIM : r - RIM + 8, part] * lev[r - RIM : r - RIM + 8, part]).astype(
                        jnp.float32
                    )
                else:
                    depth = inside(rows_n[slot, :, part])
                for k in range(levels):
                    WET[k, j, r : r + 8, :] = (depth > k + 0.5).astype(jnp.float32)
                    BOT[k, j, r : r + 8, :] = jnp.where(jnp.abs(depth - (k + 1)) < 0.5, 1.0, 0.0)
            depth = inside(
                jnp.where(
                    flat_lane < 64,
                    strips[0, r : r + 8, 3 * LANES : 4 * LANES],
                    strips[1, r : r + 8, 3 * LANES : 4 * LANES],
                )
            )
            for k in range(levels):
                WET[k, tiles - 1, r : r + 8, :] = (depth > k + 0.5).astype(jnp.float32)
                BOT[k, tiles - 1, r : r + 8, :] = jnp.where(jnp.abs(depth - (k + 1)) < 0.5, 1.0, 0.0)
        else:
            for k in range(levels):
                WET[k, :, r : r + 8, :] = jnp.zeros((tiles, 8, LANES), jnp.float32)
        for p in range(planes):
            k = p % levels
            for j in range(tiles - 1):
                part = slice(j * LANES, (j + 1) * LANES)
                if own:
                    S[p, j, r : r + 8, :] = state[p, r - RIM : r - RIM + 8, part]
                    G[p, j, r : r + 8, :] = WET[k, j, r : r + 8, :] * cot[p, r - RIM : r - RIM + 8, part]
                else:
                    if near:
                        S[p, j, r : r + 8, :] = inside(rows_s[slot, p, :, part])
                        G[p, j, r : r + 8, :] = WET[k, j, r : r + 8, :] * inside(rows_c[slot, p, :, part])
                    else:
                        outer = jnp.broadcast_to(rows_9[slot, p : p + 1, part], (8, LANES))
                        S[p, j, r : r + 8, :] = inside(outer)
            half = p // 8
            S[p, tiles - 1, r : r + 8, :] = inside(
                third(slice(half * LANES, (half + 1) * LANES), 16, p % 8)
            )
            if near:
                G[p, tiles - 1, r : r + 8, :] = WET[k, tiles - 1, r : r + 8, :] * inside(
                    third(slice(2 * LANES, 3 * LANES), 8, p)
                )

    row = lax.broadcasted_iota(jnp.int32, (tall, LANES), 0) + (lat * rows - RIM)
    turn = jnp.pi * ((row.astype(jnp.float32) + 0.5) / (rows * lat_n) - 0.5)
    COR[...] = rotation * jnp.sin(turn)

    def sweep(first, count, body):
        def run(i, carry):
            body(first + 8 * i)
            return carry

        lax.fori_loop(0, count, run, 0)

    inner = rows // 8

    def open_faces(r):
        for k in range(levels):
            wet = at(WET, k, r)
            put(OX, k, r, wet * east(wet, 1) * (courant / 60.0))
            put(OY, k, r, wet * at(WET, k, r + 1) * (courant / 60.0))

    sweep(8, inner + 2, open_faces)

    def prepare(src, step):
        def body(r):
            press = None
            for k in range(levels):
                rho = at(WET, k, r) * (
                    (-0.2 * buoyancy) * at(src, k, r) + (0.8 * buoyancy) * at(src, levels + k, r)
                )
                press = rho if press is None else press + rho
                put(PR, k, r, press)
                u = at(src, 2 * levels + k, r)
                w = 0.5 * (u + east(u, 1))
                put(W, (step * 6) * levels + k, r, w)
                square = w * w + 0.0001
                root = lax.rsqrt(square)
                put(W, (step * 6 + 1) * levels + k, r, square * root)
                put(W, (step * 6 + 2) * levels + k, r, w * root)
                w = 0.5 * (at(src, 3 * levels + k, r) + at(src, 3 * levels + k, r + 1))
                put(W, (step * 6 + 3) * levels + k, r, w)
                square = w * w + 0.0001
                root = lax.rsqrt(square)
                put(W, (step * 6 + 4) * levels + k, r, square * root)
                put(W, (step * 6 + 5) * levels + k, r, w * root)

        sweep(8, inner + 2, body)

    bands = (inner + 2) // 2
    height = 16 * bands

    def split(target, p, i, column, v):
        high = v.astype(jnp.bfloat16)
        low = (v - high.astype(jnp.float32)).astype(jnp.bfloat16)
        width = tiles * LANES
        for start, part in ((column, high), (column + width, low)):
            target[p, 16 * i : 16 * i + 16, start : start + LANES] = part

    def lon_stencils(src):
        def part(p, carry):
            for j in range(tiles):
                for i in range(bands):
                    split(QB, p, i, j * LANES, src[p, j, 8 + 16 * i : 24 + 16 * i, :])
            return carry

        lax.fori_loop(0, planes, part, 0)
        left = QB[...].reshape(planes * height, 2 * tiles * LANES)
        for t in range(tiles):
            got = jnp.dot(
                left, ahead[:, 2 * t * LANES : 2 * (t + 1) * LANES], preferred_element_type=jnp.float32
            )
            for half in range(2):
                CD[:, 2 * t + half, 8 : 8 + height, :] = got[:, half * LANES : (half + 1) * LANES].reshape(
                    planes, height, LANES
                )

    def lon_transposed(grad, step, start, bands):
        height = 16 * bands

        def part(k, carry):
            for i in range(bands):
                rows_i = slice(start + 16 * i, start + 16 * i + 16)
                base = step * 6
                ox = OX[k, :, rows_i, :]
                wx = W[base * levels + k, :, rows_i, :]
                sx = W[(base + 1) * levels + k, :, rows_i, :]
                by_speed = None
                for f in range(4):
                    p = f * levels + k
                    g = grad[p, :, rows_i, :]
                    h = ox * (east(g, 1) - g)
                    term = h * KX[step * planes + p, :, rows_i, :]
                    by_speed = term if by_speed is None else by_speed + term
                    zw = wx * h
                    zs = sx * h
                    for j in range(tiles):
                        split(ZB, p, i, j * LANES, zw[j])
                        split(ZB, p, i, (2 * tiles + j) * LANES, zs[j])
                LWX[k, :, rows_i, :] = 0.5 * (by_speed + east(by_speed, -1))
            return carry

        lax.fori_loop(0, levels, part, 0)
        left = ZB[:, :height, :].reshape(planes * height, 4 * tiles * LANES)
        for t in range(0, tiles, 2):
            stop = min(t + 2, tiles)
            got = jnp.dot(left, behind[:, t * LANES : stop * LANES], preferred_element_type=jnp.float32)
            for j in range(t, stop):
                LX[:, j, start : start + height, :] = got[:, (j - t) * LANES : (j - t + 1) * LANES].reshape(
                    planes, height, LANES
                )

    def speeds(step, k, r, along):
        base = step * 6 + 3 * along
        return [at(W, (base + i) * levels + k, r) for i in range(3)]

    def stencil(c0, c1, c2, c3, c4, c5):
        central = 37.0 * (c2 + c3) - 8.0 * (c1 + c4) + (c0 + c5)
        damping = 10.0 * (c3 - c2) - 5.0 * (c4 - c1) + (c5 - c0)
        return central, damping

    def forward(src, dst, step, first, count):
        prepare(src, step)
        lon_stencils(src)

        def body(r):
            turn = COR[pl.ds(r, 8), :][None]

            def level(k, carry):
                wet = at(WET, k, r)
                ox = at(OX, k, r)
                oy = at(OY, k, r)
                wx, sx, tx = speeds(step, k, r, 0)
                wy, sy, ty = speeds(step, k, r, 1)
                lo = jnp.maximum(k - 1, 0)
                hi = jnp.minimum(k + 1, levels - 1)
                mix_lo = vert_mix * at(WET, lo, r)
                mix_hi = vert_mix * at(WET, hi, r)
                for f in range(4):
                    p = f * levels + k
                    q = at(src, p, r)
                    c = CD[p, :tiles, pl.ds(r, 8), :]
                    d = CD[p, tiles:, pl.ds(r, 8), :]
                    put(KX, step * planes + p, r, c - tx * d)
                    flux = ox * (wx * c - sx * d)
                    total = q - (flux - east(flux, -1))
                    c, d = stencil(*[at(src, p, r + o) for o in (-2, -1)], q, *[at(src, p, r + o) for o in (1, 2, 3)])
                    put(KY, step * planes + p, r, c - ty * d)
                    flux = oy * (wy * c - sy * d)
                    put(FA, p, r, flux)
                    total = total - (flux - at(FA, p, r - 1))
                    total = total + mix_lo * (at(src, f * levels + lo, r) - q)
                    total = total + mix_hi * (at(src, f * levels + hi, r) - q)
                    if f == 2:
                        press = at(PR, k, r)
                        total = total + turn * at(src, 3 * levels + k, r)
                        total = total - 0.5 * (east(press, 1) - east(press, -1))
                        total = total - bottom_drag * at(BOT, k, r) * q
                    if f == 3:
                        total = total - turn * at(src, 2 * levels + k, r)
                        total = total - 0.5 * (at(PR, k, r + 1) - at(PR, k, r - 1))
                        total = total - bottom_drag * at(BOT, k, r) * q
                    put(dst, p, r, wet * total)
                return carry

            lax.fori_loop(0, levels, level, 0)

        sweep(first, count, body)

    def backward(grad, step, first_face, faces, first, count, store):
        def face_body(r):
            def level(k, carry):
                oy = at(OY, k, r)
                wy, sy, _ = speeds(step, k, r, 1)
                by_speed = None
                for f in range(4):
                    p = f * levels + k
                    h = oy * (at(grad, p, r + 1) - at(grad, p, r))
                    put(FA, p, r, wy * h)
                    put(FB, p, r, sy * h)
                    term = h * at(KY, step * planes + p, r)
                    by_speed = term if by_speed is None else by_speed + term
                put(LWY, k, r, by_speed)
                return carry

            lax.fori_loop(0, levels, level, 0)

        sweep(first_face, faces, face_body)
        lon_transposed(grad, step, 8 if step else RIM, (inner + 2 if step else inner) // 2)

        def body(r):
            turn = COR[pl.ds(r, 8), :][None]

            def level(i, below):
                k = levels - 1 - i
                wet = at(WET, k, r)
                lo = jnp.maximum(k - 1, 0)
                hi = jnp.minimum(k + 1, levels - 1)
                mix_wet = vert_mix * wet
                wet_lo = jnp.where(k > 0, 1.0, 0.0) * vert_mix * at(WET, lo, r)
                wet_hi = jnp.where(k < levels - 1, 1.0, 0.0) * vert_mix * at(WET, hi, r)
                has_lo = jnp.where(k > 0, 1.0, 0.0) * mix_wet
                has_hi = jnp.where(k < levels - 1, 1.0, 0.0) * mix_wet
                keep = 1.0 - wet_lo - wet_hi
                gu = at(grad, 2 * levels + k, r)
                gv = at(grad, 3 * levels + k, r)
                by_press = 0.5 * (east(gu, 1) - east(gu, -1)) + 0.5 * (
                    at(grad, 3 * levels + k, r + 1) - at(grad, 3 * levels + k, r - 1)
                )
                below = below + by_press
                by_rho = buoyancy * wet * below
                drag = bottom_drag * at(BOT, k, r)
                sums = []
                for f in range(4):
                    p = f * levels + k
                    g = at(grad, p, r)
                    total = keep * g + has_lo * at(grad, f * levels + lo, r) + has_hi * at(grad, f * levels + hi, r)
                    total = total + at(LX, p, r)
                    z = [at(FA, p, r + o) for o in range(-3, 3)]
                    total = total + (37.0 * (z[2] + z[3]) - 8.0 * (z[1] + z[4]) + (z[0] + z[5]))
                    z = [at(FB, p, r + o) for o in range(-3, 3)]
                    total = total + (10.0 * (z[3] - z[2]) - 5.0 * (z[4] - z[1]) + (z[5] - z[0]))
                    sums.append(total)
                speed_y = at(LWY, k, r) + at(LWY, k, r - 1)
                sums[0] = sums[0] - 0.2 * by_rho
                sums[1] = sums[1] + 0.8 * by_rho
                sums[2] = sums[2] + at(LWX, k, r) - turn * gv - drag * gu
                sums[3] = sums[3] + 0.5 * speed_y + turn * gu - drag * gv
                for f in range(4):
                    store(f * levels + k, r, sums[f], wet)
                return below

            lax.fori_loop(0, levels, level, jnp.zeros((tiles, 8, LANES), jnp.float32))

        sweep(first, count, body)

    forward(S, X1, 0, 8, inner + 2)
    forward(X1, X2, 1, RIM - 4, inner + 1)

    def store_middle(p, r, v, wet):
        put(A1, p, r, wet * v)

    def store_last(p, r, v, wet):
        row = pl.multiple_of(r - RIM, 8)
        for j in range(tiles - 1):
            adjoint[p, pl.ds(row, 8), j * LANES : (j + 1) * LANES] = v[j]

    backward(G, 1, 8, inner + 2, RIM - 4, inner + 1, store_middle)
    backward(A1, 0, RIM - 4, inner + 1, RIM, inner, store_last)
    for p in range(planes):
        for j in range(tiles - 1):
            final[p, :, j * LANES : (j + 1) * LANES] = X2[p, j, RIM : RIM + rows, :]


def band_matrices(width):
    central = np.zeros((width, width), np.float32)
    damping = np.zeros((width, width), np.float32)
    face = np.arange(width)
    for offset, c, d in ((-2, 1, -1), (-1, -8, 5), (0, 37, -10), (1, 37, 10), (2, -8, -5), (3, 1, 1)):
        central[(face + offset) % width, face] = c
        damping[(face + offset) % width, face] = d
    both = np.concatenate([central, damping], axis=1)
    ahead = np.concatenate([both, both], axis=0)
    behind = np.concatenate([central.T, central.T, -damping.T, -damping.T], axis=0)
    return jnp.asarray(ahead, jnp.bfloat16), jnp.asarray(behind, jnp.bfloat16)


def steps(lat_n, state, cot, sea, lev, halos):
    planes, rows, cols = state.shape
    levels = planes // 4
    f32 = jnp.float32
    tall = rows + 2 * RIM
    tiles = cols // LANES + 1

    def scratch(count):
        return pltpu.VMEM((count, tiles, tall, LANES), f32)

    width = tiles * LANES
    height = rows + 16
    shapes = [scratch(count) for count in [planes] * 8 + [2 * planes] * 2]
    shapes.append(pltpu.VMEM((planes, 2 * tiles, tall, LANES), f32))
    shapes += [scratch(count) for count in [levels] * 5 + [12 * levels, levels, levels]]
    shapes.append(pltpu.VMEM((tall, LANES), f32))
    shapes.append(pltpu.VMEM((planes, height, 2 * width), jnp.bfloat16))
    shapes.append(pltpu.VMEM((planes, height, 4 * width), jnp.bfloat16))
    return pl.pallas_call(
        functools.partial(step_kernel, lat_n),
        out_shape=(jax.ShapeDtypeStruct(state.shape, f32),) * 2,
        in_specs=[pl.BlockSpec(memory_space=pltpu.VMEM)] * 11,
        out_specs=(pl.BlockSpec(memory_space=pltpu.VMEM),) * 2,
        scratch_shapes=shapes,
        compiler_params=pltpu.CompilerParams(vmem_limit_bytes=56 * 1024 * 1024),
        name="steps",
    )(state, cot, sea, lev, *halos, *band_matrices(width))


def shards(state, cotangent, seamask, levels):
    shape = state.shape
    flat = (shape[0] * shape[1], shape[2], shape[3])
    state = state.reshape(flat)
    cotangent = cotangent.reshape(flat)
    halos = exchange(state, cotangent, seamask, levels)
    final, adjoint = steps(lax.axis_size("lat"), state, cotangent, seamask, levels, halos)
    return (final.reshape(shape), adjoint.reshape(shape))


def solution(mesh):
    placed = (
        P(None, None, "lat", "lon"),
        P(None, None, "lat", "lon"),
        P("lat", "lon"),
        P("lat", "lon"),
    )
    return jax.shard_map(
        shards,
        mesh=mesh,
        in_specs=placed,
        out_specs=(P(None, None, "lat", "lon"), P(None, None, "lat", "lon")),
        check_vma=False,
    )
```
